32 devices in a mesh: section: 2 (over core), seq: 8 (over z, x), fsdp: 2 (over y).
Axes of the slice: x: 2, y: 2, z: 4, core: 2. Of those that a mesh axis runs over, the one named last changes fastest.
Arguments:
- tokens: bfloat16 [8, 2048, 640], P('fsdp', 'seq'), may hold values from -6 to 6
- layer_inputs: bfloat16 [2, 8, 2048, 256], P('section', 'fsdp', 'seq'), may hold values from -6 to 6
- doc_lengths: int32 [8, 4], P('fsdp'), may hold values from 1 to 2045, as said below
- order: int32 [2, 4], P('fsdp'), may hold values from 0 to 3, each once within a row
- out_grad: bfloat16 [8, 2048, 640], P('fsdp', 'seq'), may hold values from -6 to 6
- query_weight: bfloat16 [2, 640, 1024], P('section', ('seq', 'fsdp')), may hold values from -0.25 to 0.25
- key_weight: bfloat16 [2, 640, 256], P('section', ('seq', 'fsdp')), may hold values from -0.25 to 0.25
- value_weight: bfloat16 [2, 640, 256], P('section', ('seq', 'fsdp')), may hold values from -0.25 to 0.25
- output_weight: bfloat16 [2, 1024, 640], P('section', None, ('seq', 'fsdp')), may hold values from -0.1875 to 0.1875
- gate_weight: bfloat16 [2, 640, 2048], P('section', ('seq', 'fsdp')), may hold values from -0.25 to 0.25
- up_weight: bfloat16 [2, 640, 2048], P('section', ('seq', 'fsdp')), may hold values from -0.25 to 0.25
- down_weight: bfloat16 [2, 2048, 640], P('section', None, ('seq', 'fsdp')), may hold values from -0.125 to 0.125
- lowrank_down: bfloat16 [2, 640, 64], P('section', ('seq', 'fsdp')), may hold values from -0.25 to 0.25
- lowrank_up: bfloat16 [2, 64, 640], P('section', None, ('seq', 'fsdp')), may hold values from -0.75 to 0.75
- input_gate: bfloat16 [2, 640, 256], P('section', ('seq', 'fsdp')), may hold values from -0.25 to 0.25
- input_proj: bfloat16 [2, 256, 640], P('section', None, ('seq', 'fsdp')), may hold values from -0.375 to 0.375
- norm_gains: bfloat16 [2, 5, 640], P('section', None, ('seq', 'fsdp')), may hold values from 0.25 to 1.75
- qk_gains: bfloat16 [2, 2, 256], P('section', None, ('seq', 'fsdp')), may hold values from 0.25 to 1.75
Outputs:
- activations: bfloat16 [2, 8, 2048, 640], P('section', 'fsdp', 'seq')
- input_grads: bfloat16 [2, 8, 2048, 640], P('section', 'fsdp', 'seq')
- grad_query: float32 [2, 640, 1024], P('section', ('seq', 'fsdp'))
- grad_key: float32 [2, 640, 256], P('section', ('seq', 'fsdp'))
- grad_value: float32 [2, 640, 256], P('section', ('seq', 'fsdp'))
- grad_output: float32 [2, 1024, 640], P('section', None, ('seq', 'fsdp'))
- grad_gate: float32 [2, 640, 2048], P('section', ('seq', 'fsdp'))
- grad_up: float32 [2, 640, 2048], P('section', ('seq', 'fsdp'))
- grad_down: float32 [2, 2048, 640], P('section', None, ('seq', 'fsdp'))
- grad_lowrank_down: float32 [2, 640, 64], P('section', ('seq', 'fsdp'))
- grad_lowrank_up: float32 [2, 64, 640], P('section', None, ('seq', 'fsdp'))
- grad_input_gate: float32 [2, 640, 256], P('section', ('seq', 'fsdp'))
- grad_input_proj: float32 [2, 256, 640], P('section', None, ('seq', 'fsdp'))
- grad_norm_gains: float32 [2, 5, 640], P('section', None, ('seq', 'fsdp'))
- grad_qk_gains: float32 [2, 2, 256], P('section', None, ('seq', 'fsdp'))
The draws below stay inside these ranges and needn't reach their ends.
Inputs may be any that keep to these rules, and one draw needn't show every extreme that they name: `doc_lengths`: each row lists 4 document lengths that sum to 2048; in every group of 4 rows (one index of fsdp) one row, chosen by the seed, is a document of 2045 tokens followed by 4 - 1 documents of one token. `order`: each row is an ordering of the group's micro-batches.
All inputs are finite; a program needn't handle non-finite values.
Results may differ from the reference program's by a relative error of at most 0.029.
Values may be sent and summed in bfloat16 or wider, within the bound.
No kernel may reach another device: no remote copies, remote signals or barrier semaphores. Data moves between devices by JAX's collectives and lax.ppermute only.
A program may use at most 320 MiB of HBM per device.

```python
import jax
import jax.numpy as jnp
from jax import lax

D = 640
FF = 2048
HEADS = 4
KV_HEADS = 1
HD = 256
WINDOW = 512
RANK = 64
PLI = 256
MB = 4
DOCS = 4
SEQ = 2048
MB_ALL = 8
GROUPS = 2


def draw_doc_lengths(key, part):
    key = jax.random.fold_in(key, 11)
    row_keys = jax.random.split(jax.random.fold_in(key, 1), MB_ALL)

    def one_row(row_key):
        cuts = jax.random.permutation(row_key, SEQ - 1)[:DOCS - 1].astype(jnp.int32) + 1
        cuts = jnp.sort(cuts)
        bounds = jnp.concatenate([jnp.zeros((1,), jnp.int32), cuts, jnp.full((1,), SEQ, jnp.int32)])
        return bounds[1:] - bounds[:-1]
    ragged = jax.vmap(one_row)(row_keys)
    long_row = jnp.concatenate([jnp.full((1,), SEQ - DOCS + 1, jnp.int32), jnp.ones((DOCS - 1,), jnp.int32)])
    chosen = jax.random.randint(jax.random.fold_in(key, 2), (MB_ALL // MB,), 0, MB)
    row_ids = jnp.arange(MB_ALL, dtype=jnp.int32)
    is_long = row_ids % MB == chosen[row_ids // MB]
    return jnp.where(is_long[:, None], long_row[None, :], ragged).astype(jnp.int32)


def raised(values, own_key, source, target, blocks, factor):
    def block_of(axis_at):
        return (jnp.arange(values.shape[axis_at]) // (values.shape[axis_at] // blocks)).reshape((-1,) + (1,) * (values.ndim - 1 - axis_at))

    first = jax.random.permutation(own_key, blocks)[block_of(target)]
    other_side = (block_of(target) + blocks // 2) % blocks
    return jnp.where((block_of(source) == first) | (block_of(source) == other_side), factor * values, values)


def steps_of(own_key, dims, shards, least, high):
    def one(position, blocks):
        heights = jax.random.uniform(jax.random.fold_in(jax.random.fold_in(own_key, 6), position), (blocks,), jnp.float32, least / len(shards), high / len(shards))
        return jnp.repeat(jnp.exp(heights), dims[position] // blocks).reshape((-1,) + (1,) * (len(dims) - position - 1))

    loudness = one(*shards[0])
    for cut in shards[1:]:
        loudness = loudness * one(*cut)
    return loudness


def gaussian(rng, extent, scale, limit, pieces=(), kind=jnp.bfloat16):
    gain = steps_of(rng, extent, pieces, -0.22, 0.18) if pieces else 1.0
    entries = jax.random.normal(rng, extent, jnp.float32) * scale * gain
    return jnp.minimum(jnp.maximum(entries, -limit), limit).astype(kind)


def heavy_noise(own_key, shape, width, most, cuts, heavy, kind=jnp.bfloat16):
    result = width * jax.random.normal(own_key, shape, jnp.float32)
    if cuts:
        result = result * steps_of(own_key, shape, cuts, -0.22, 0.18)
    return jnp.clip(raised(result, jax.random.fold_in(own_key, 3), *heavy), -most, most).astype(kind)


def setup_inputs(seed: int = 0) -> dict:
    keys = jax.random.split(jax.random.key(seed), 19)
    return {
        "tokens": gaussian(keys[0], (MB_ALL, SEQ, D), 1.0, 6.0, ((0, 2), (1, 8))),
        "layer_inputs": gaussian(keys[1], (2, MB_ALL, SEQ, PLI), 1.0, 6.0, ((0, 2), (1, 2), (2, 8))),
        "doc_lengths": draw_doc_lengths(jax.random.fold_in(keys[18], 71), 0),
        "order": jax.vmap(lambda own: jax.random.permutation(own, MB))(jax.random.split(keys[3], GROUPS)).reshape((GROUPS, MB)).astype(jnp.int32),
        "out_grad": heavy_noise(keys[4], (MB_ALL, SEQ, D), 1.0, 6.0, ((0, 2), (1, 8)), (1, 2, 8, 2.0)),
        "query_weight": gaussian(keys[5], (2, D, HEADS * HD), D ** -0.5, 0.25, ((0, 2), (1, 16))),
        "key_weight": gaussian(keys[6], (2, D, KV_HEADS * HD), D ** -0.5, 0.25, ((0, 2), (1, 16))),
        "value_weight": gaussian(keys[7], (2, D, KV_HEADS * HD), D ** -0.5, 0.25, ((0, 2), (1, 16))),
        "output_weight": gaussian(keys[8], (2, HEADS * HD, D), (HEADS * HD) ** -0.5, 0.1875, ((0, 2), (2, 16))),
        "gate_weight": gaussian(keys[9], (2, D, FF), D ** -0.5, 0.25, ((0, 2), (1, 16))),
        "up_weight": gaussian(keys[10], (2, D, FF), D ** -0.5, 0.25, ((0, 2), (1, 16))),
        "down_weight": gaussian(keys[11], (2, FF, D), FF ** -0.5, 0.125, ((0, 2), (2, 16))),
        "lowrank_down": gaussian(keys[12], (2, D, RANK), D ** -0.5, 0.25, ((0, 2), (1, 16))),
        "lowrank_up": gaussian(keys[13], (2, RANK, D), RANK ** -0.5, 0.75, ((0, 2), (2, 16))),
        "input_gate": gaussian(keys[14], (2, D, PLI), D ** -0.5, 0.25, ((0, 2), (1, 16))),
        "input_proj": gaussian(keys[15], (2, PLI, D), PLI ** -0.5, 0.375, ((0, 2), (2, 16))),
        "norm_gains": jnp.clip(1.0 + 0.15 * jax.random.normal(keys[16], (2, 5, D), jnp.float32), 0.25, 1.75).astype(jnp.bfloat16),
        "qk_gains": jnp.clip(1.0 + 0.15 * jax.random.normal(keys[17], (2, 2, HD), jnp.float32), 0.25, 1.75).astype(jnp.bfloat16),
    }


epsilon = 1e-06
rope_base = 10000.0
masked_score = -1e+30

@jax.custom_vjp
def low(v):
    return lax.optimization_barrier(v.astype(jnp.bfloat16)).astype(jnp.float32)

@jax.custom_vjp
def low_back(v):
    return v

def low_keep(v):
    return (low(v), None)

def low_pass(kept, grad):
    return (grad,)

def back_keep(v):
    return (v, None)

def back_low(kept, grad):
    return (low(grad),)
low.defvjp(low_keep, low_pass)
low_back.defvjp(back_keep, back_low)

def product(left, right):
    return jnp.dot(left, right, preferred_element_type=jnp.float32, precision=lax.Precision.HIGHEST)

def rms_scale(values_in, gain_row):
    return values_in * lax.rsqrt(lax.optimization_barrier(jnp.mean(values_in * values_in, axis=-1, keepdims=True)) + epsilon) * gain_row

def gelu_times(gate_in, other_in):
    return jax.nn.gelu(gate_in, approximate=True) * other_in

def rope_tables(offsets, head_width):
    inverse = rope_base ** (-(jnp.arange(head_width // 2, dtype=jnp.float32) * 2.0 / head_width))
    angles = offsets.astype(jnp.float32)[:, None] * inverse[None, :]
    angles = jnp.concatenate([angles, angles], axis=1)
    return (jnp.cos(angles)[:, None, :], jnp.sin(angles)[:, None, :])

def rotate(values_in, cosines, sines):
    half_width = values_in.shape[-1] // 2
    turned = jnp.concatenate([-values_in[..., half_width:], values_in[..., :half_width]], axis=-1)
    return values_in * cosines + turned * sines

def head_path(pre_heads, gain_row, cosines, sines, factor):
    shaped = pre_heads.reshape(pre_heads.shape[0], -1, gain_row.shape[0])
    return rotate(rms_scale(shaped, gain_row), cosines, sines) * factor

def doc_numbers(lengths, positions):
    ends = jnp.cumsum(lengths).astype(jnp.int32)
    return lax.optimization_barrier(jnp.sum((positions[:, None] >= ends[None, :]).astype(jnp.int32), axis=1)).astype(jnp.int32)

def doc_offsets(lengths, positions):
    ends = jnp.cumsum(lengths).astype(jnp.int32)
    passed = positions[:, None] >= ends[None, :]
    starts = lax.optimization_barrier(jnp.sum(jnp.where(passed, lengths[None, :], 0), axis=1)).astype(jnp.int32)
    return (positions - starts).astype(jnp.int32)

def attention(queries, keys_low, values, docs):
    total_rows, head_count, head_width = queries.shape
    kv_heads = keys_low.shape[1]
    rows_block = min(512, total_rows)
    key_span = rows_block + WINDOW
    pad_keys = jnp.concatenate([jnp.zeros((WINDOW, kv_heads, head_width), jnp.float32), keys_low], axis=0)
    pad_values = jnp.concatenate([jnp.zeros((WINDOW, kv_heads, head_width), jnp.float32), values], axis=0)
    pad_docs = jnp.concatenate([jnp.full((WINDOW,), -1, jnp.int32), docs]).astype(jnp.int32)
    starts = (jnp.arange(total_rows // rows_block, dtype=jnp.int32) * rows_block).astype(jnp.int32)

    def one_block(start):
        query_block = lax.dynamic_slice_in_dim(queries, start, rows_block, 0)
        key_block = lax.dynamic_slice_in_dim(pad_keys, start, key_span, 0)
        value_block = lax.dynamic_slice_in_dim(pad_values, start, key_span, 0)
        query_docs = lax.dynamic_slice_in_dim(docs, start, rows_block, 0)
        key_docs = lax.dynamic_slice_in_dim(pad_docs, start, key_span, 0)
        distance_pos = jnp.arange(rows_block, dtype=jnp.int32)[:, None] + WINDOW - jnp.arange(key_span, dtype=jnp.int32)[None, :]
        allowed_pairs = (distance_pos >= 0) & (distance_pos < WINDOW) & (query_docs[:, None] == key_docs[None, :])
        grouped = query_block.reshape(rows_block, kv_heads, head_count // kv_heads, head_width)
        scores = low_back(jnp.einsum('tkgd,ckd->kgtc', grouped, key_block, precision=lax.Precision.HIGHEST))
        soft_weights = low(jax.nn.softmax(jnp.where(allowed_pairs, scores, masked_score), axis=-1))
        mixed = jnp.einsum('kgtc,ckd->tkgd', soft_weights, value_block, precision=lax.Precision.HIGHEST)
        return mixed.reshape(rows_block, head_count * head_width)
    blocks = lax.map(jax.checkpoint(one_block), starts)
    return blocks.reshape(total_rows, head_count * head_width)

def layer(inputs, extra_row, lengths, params):
    query_w, key_w, value_w, output_w, gate_w, up_w, down_w, lowrank_a, lowrank_b, gate_in_w, proj_in_w, gains, qk_gain = params
    head_width = qk_gain.shape[1]
    total_rows = inputs.shape[0]
    positions = jnp.arange(total_rows, dtype=jnp.int32)
    docs = doc_numbers(lengths, positions)
    cosines, sines = rope_tables(doc_offsets(lengths, positions), head_width)
    normed = low(rms_scale(inputs, gains[0]))
    q_pre = low_back(product(normed, query_w))
    k_pre = low_back(product(normed, key_w))
    values = low_back(low(product(normed, value_w))).reshape(total_rows, -1, head_width)
    queries = low(head_path(q_pre, qk_gain[0], cosines, sines, head_width ** (-0.5)))
    keys_low = low(head_path(k_pre, qk_gain[1], cosines, sines, 1.0))
    mixed = low_back(low(attention(queries, keys_low, values, docs)))
    attn_out = low_back(product(mixed, output_w))
    lowrank_mid = low_back(low(product(normed, lowrank_a)))
    lowrank_out = low_back(product(lowrank_mid, lowrank_b))
    first_sum = inputs + rms_scale(attn_out, gains[1]) + lowrank_out
    normed_two = low(rms_scale(first_sum, gains[2]))
    gate_proj = low_back(product(normed_two, gate_w))
    up_proj = low_back(product(normed_two, up_w))
    hidden = low(gelu_times(gate_proj, up_proj))
    ff_out = low_back(product(hidden, down_w))
    second_sum = first_sum + rms_scale(ff_out, gains[3])
    pli_gate = low_back(product(low(second_sum), gate_in_w))
    pli_mix = low(gelu_times(pli_gate, extra_row))
    pli_out = low_back(product(pli_mix, proj_in_w))
    return second_sum + rms_scale(pli_out, gains[4])

def reference(tokens, layer_inputs, doc_lengths, order, out_grad, query_weight, key_weight, value_weight, output_weight, gate_weight, up_weight, down_weight, lowrank_down, lowrank_up, input_gate, input_proj, norm_gains, qk_gains):
    stacks = tuple((piece.astype(jnp.float32) for piece in (query_weight, key_weight, value_weight, output_weight, gate_weight, up_weight, down_weight, lowrank_down, lowrank_up, input_gate, input_proj, norm_gains, qk_gains)))
    micro_count = order.shape[1]
    run_count = order.shape[0] * micro_count

    def one_run(totals, index):
        group = index // micro_count
        seq_id = (group * micro_count + order[group, index % micro_count]).astype(jnp.int32)
        inputs = tokens[seq_id].astype(jnp.float32)
        lengths = doc_lengths[seq_id]
        extra_first = layer_inputs[0, seq_id].astype(jnp.float32)
        extra_second = layer_inputs[1, seq_id].astype(jnp.float32)
        first_params = tuple((piece[0] for piece in stacks))
        second_params = tuple((piece[1] for piece in stacks))

        def both_layers(inputs_in, offset_in, params_a, params_b):
            middle = low_back(low(layer(inputs_in, extra_first, lengths, params_a)) + offset_in)
            return (middle, layer(middle, extra_second, lengths, params_b))
        (middle, last), pull = jax.vjp(both_layers, inputs, jnp.zeros_like(inputs), first_params, second_params)
        grad_inputs, grad_middle, grads_a, grads_b = pull((jnp.zeros_like(middle), out_grad[index].astype(jnp.float32)))
        new_totals = tuple((total + jnp.stack([part_a, part_b]) for total, part_a, part_b in zip(totals, grads_a, grads_b)))
        return (new_totals, (middle.astype(jnp.bfloat16), last.astype(jnp.bfloat16), grad_inputs.astype(jnp.bfloat16), grad_middle.astype(jnp.bfloat16)))
    zeros = tuple((jnp.zeros_like(piece) for piece in stacks))
    totals, (middles, lasts, grads_first, grads_second) = lax.scan(one_run, zeros, jnp.arange(run_count, dtype=jnp.int32))
    activations = jnp.stack([middles, lasts])
    input_grads = jnp.stack([grads_first, grads_second])
    return (activations, input_grads, totals[0], totals[1], totals[2], totals[3], totals[4], totals[5], totals[6], totals[7], totals[8], totals[9], totals[10], totals[11], totals[12])
```

```python
import jax
import jax.numpy as jnp
from jax import lax
from jax.sharding import PartitionSpec as P

WINDOW = 512

epsilon = 1e-06
rope_base = 10000.0
masked_score = -1e30
low = jnp.bfloat16


def product(left, right):
    return jnp.dot(left, right, preferred_element_type=jnp.float32)


def product_tn(left, right):
    return lax.dot_general(
        left, right, (((0,), (0,)), ((), ())), preferred_element_type=jnp.float32
    )


def product_nt(left, right):
    return lax.dot_general(
        left, right, (((1,), (1,)), ((), ())), preferred_element_type=jnp.float32
    )


def swap_cores(value):
    return lax.ppermute(value, "section", [(0, 1), (1, 0)])


def from_behind(value, steps):
    count = lax.axis_size("seq")
    leading, last = (max(0, -steps), min(count, count - steps))
    return lax.ppermute(value, "seq", [(source, source + steps) for source in range(leading, last)])


def index_bits():
    bits = []
    for axis in ("seq", "fsdp"):
        count = lax.axis_size(axis)
        assert count & (count - 1) == 0
        distance = count // 2
        while distance:
            bits.append((axis, distance))
            distance //= 2
    return bits


def partner_swap(value, bit):
    axis, distance = bit
    count = lax.axis_size(axis)
    return lax.ppermute(value, axis, [(i, i ^ distance) for i in range(count)])


def stage_orders():
    bits = index_bits()
    seq_places = [i for i, b in enumerate(bits) if b[0] == "seq"]
    fsdp_places = [i for i, b in enumerate(bits) if b[0] == "fsdp"]
    far, near = seq_places[:-1], seq_places[-1:]
    return (
        far + near + fsdp_places,
        far + fsdp_places + near,
        near + fsdp_places + far,
    )


def gather_rows(shard, order):
    bits = index_bits()
    value = shard.reshape((1,) * len(bits) + shard.shape)
    for place in order:
        value = jnp.concatenate([value, partner_swap(value, bits[place])], axis=place)
    return value.reshape(-1, shard.shape[-1])


def scatter_rows(whole, order):
    bits = index_bits()
    rows = whole.shape[0] >> len(bits)
    value = whole.reshape((2,) * len(bits) + (rows, whole.shape[-1]))
    for at, place in enumerate(reversed(order)):
        kept = lax.slice_in_dim(value, 0, 1, axis=place)
        sent = lax.slice_in_dim(value, 1, 2, axis=place)
        value = kept.astype(jnp.float32) + partner_swap(sent, bits[place]).astype(jnp.float32)
        if at < len(order) - 1:
            value = value.astype(low)
    return value.reshape(rows, -1)


def rms_scale(values_in, gain_row):
    return (
        values_in
        * lax.rsqrt(jnp.mean(values_in * values_in, axis=-1, keepdims=True) + epsilon)
        * gain_row
    )


def norm_back(values_in, gain_row, grad_out):
    result, pull = jax.vjp(rms_scale, values_in, gain_row)
    return pull(grad_out)


def gelu_times(gate_in, other_in):
    return jax.nn.gelu(gate_in, approximate=True) * other_in


def rotate(values_in, cosines, sines):
    half_width = values_in.shape[-1] // 2
    turned = jnp.concatenate([-values_in[..., half_width:], values_in[..., :half_width]], axis=-1)
    return values_in * cosines + turned * sines


def head_path(pre_heads, gain_row, cosines, sines, factor):
    shaped = pre_heads.reshape(pre_heads.shape[0], -1, gain_row.shape[0])
    return rotate(rms_scale(shaped, gain_row), cosines, sines) * factor


def doc_numbers(ends, positions):
    return jnp.sum((positions[..., :, None] >= ends[..., None, :]).astype(jnp.int32), axis=-1)


def attention_probs(queries, window_keys, pair_mask):
    scores = jnp.einsum("ithd,icd->ihtc", queries, window_keys, preferred_element_type=jnp.float32)
    return jax.nn.softmax(jnp.where(pair_mask[:, None], scores, masked_score), axis=-1)


def fetch_edges(pair, hops):
    slots = [from_behind(pair, distance) for distance in range(hops, 0, -1)]
    return jnp.concatenate(slots + [pair], axis=1)


def return_edges(grad_pair, hops, rows_here):
    own = grad_pair[:, hops * rows_here :]
    for distance in range(1, hops + 1):
        start = (hops - distance) * rows_here
        own = own + from_behind(
            grad_pair[:, start : start + rows_here].astype(low), -distance
        ).astype(jnp.float32)
    return own


def layer_forward(inputs, extra, w, shared):
    cosines, sines, pair_mask, steps, rows_here, hops = shared
    g = w["gains"]
    head_width = w["qk"].shape[1]
    rows = inputs.shape[0]
    normed = rms_scale(inputs, g[0]).astype(low)
    pair_pre = product(normed, w["kv"])
    k_pre = pair_pre[:, :head_width]
    values = pair_pre[:, head_width:].astype(low)
    keys_low = head_path(k_pre, w["qk"][1], cosines, sines, 1.0).astype(low).reshape(rows, -1)
    window = fetch_edges(
        jnp.concatenate([keys_low, values], axis=1).reshape(steps, rows_here, -1), hops
    )
    q_pre = jnp.concatenate([product(normed, part) for part in w["q"]], axis=1)
    queries = head_path(q_pre, w["qk"][0], cosines, sines, head_width ** (-0.5)).astype(low)
    lowrank_mid = product(normed, w["lrd"]).astype(low)
    queries = queries.reshape(steps, rows_here, -1, head_width)
    window_keys, window_values = window[..., :head_width], window[..., head_width:]
    probs = attention_probs(queries, window_keys, pair_mask)
    mixed = (
        jnp.einsum(
            "ihtc,icd->ithd", probs.astype(low), window_values, preferred_element_type=jnp.float32
        )
        .astype(low)
        .reshape(rows, -1)
    )
    half = mixed.shape[1] // 2
    attn_out = product_nt(mixed[:, :half], w["o"][0]) + product_nt(mixed[:, half:], w["o"][1])
    first_sum = inputs + rms_scale(attn_out, g[1]) + product_nt(lowrank_mid, w["lru"])
    normed_two = rms_scale(first_sum, g[2]).astype(low)
    gates = [product(normed_two, part) for part in w["gate"]]
    ups = [product(normed_two, part) for part in w["up"]]
    hiddens = [gelu_times(a, b).astype(low) for a, b in zip(gates, ups)]
    ff_out = product_nt(hiddens[0], w["down"][0]) + product_nt(hiddens[1], w["down"][1])
    second_sum = first_sum + rms_scale(ff_out, g[3])
    second_low = second_sum.astype(low)
    pli_gate = product(second_low, w["ig"])
    pli_mix = gelu_times(pli_gate, extra).astype(low)
    pli_out = product_nt(pli_mix, w["ip"])
    result = second_sum + rms_scale(pli_out, g[4])
    saved = dict(
        inputs=inputs,
        normed=normed,
        q_pre=q_pre,
        k_pre=k_pre,
        queries=queries,
        window_keys=window_keys,
        window_values=window_values,
        probs=probs,
        mixed=mixed,
        attn_out=attn_out,
        lowrank_mid=lowrank_mid,
        first_sum=first_sum,
        normed_two=normed_two,
        gates=gates,
        ups=ups,
        hiddens=hiddens,
        ff_out=ff_out,
        second_low=second_low,
        pli_gate=pli_gate,
        pli_mix=pli_mix,
        pli_out=pli_out,
    )
    return result, saved


def layer_backward(grad_result, extra, w, saved, shared):
    cosines, sines, pair_mask, steps, rows_here, hops = shared
    g = w["gains"]
    head_width = w["qk"].shape[1]
    s = saved
    rows = grad_result.shape[0]
    out = {}
    grad_pli_out, gain_four = norm_back(s["pli_out"], g[4], grad_result)
    grad_pli_out = grad_pli_out.astype(low)
    grad_mix = product(grad_pli_out, w["ip"])
    _, pull_mix = jax.vjp(gelu_times, s["pli_gate"], extra)
    grad_pli_gate = pull_mix(grad_mix)[0].astype(low)
    out["ip"] = product_tn(grad_pli_out, s["pli_mix"])
    out["ig"] = product_tn(s["second_low"], grad_pli_gate)
    grad_second = grad_result + product_nt(grad_pli_gate, w["ig"])
    grad_ff_out, gain_three = norm_back(s["ff_out"], g[3], grad_second)
    grad_ff_out = grad_ff_out.astype(low)
    out["down"] = [product_tn(grad_ff_out, part) for part in s["hiddens"]]
    grad_gates, grad_ups = [], []
    for at in range(2):
        grad_hidden = product(grad_ff_out, w["down"][at])
        _, pull = jax.vjp(gelu_times, s["gates"][at], s["ups"][at])
        one, two = pull(grad_hidden)
        grad_gates.append(one.astype(low))
        grad_ups.append(two.astype(low))
    out["gate"] = [product_tn(s["normed_two"], part) for part in grad_gates]
    out["up"] = [product_tn(s["normed_two"], part) for part in grad_ups]
    grad_normed_two = (
        product_nt(grad_gates[0], w["gate"][0])
        + product_nt(grad_gates[1], w["gate"][1])
        + product_nt(grad_ups[0], w["up"][0])
        + product_nt(grad_ups[1], w["up"][1])
    )
    grad_first, gain_two = norm_back(s["first_sum"], g[2], grad_normed_two)
    grad_first = grad_first + grad_second
    grad_attn, gain_one = norm_back(s["attn_out"], g[1], grad_first)
    grad_attn = grad_attn.astype(low)
    grad_lowrank_out = grad_first.astype(low)
    half = s["mixed"].shape[1] // 2
    out["o"] = [
        product_tn(grad_attn, s["mixed"][:, :half]),
        product_tn(grad_attn, s["mixed"][:, half:]),
    ]
    grad_mixed = jnp.concatenate([product(grad_attn, part) for part in w["o"]], axis=1).astype(low)
    grad_heads = grad_mixed.reshape(steps, rows_here, -1, head_width)
    probs = s["probs"]
    grad_values_win = jnp.einsum(
        "ihtc,ithd->icd", probs.astype(low), grad_heads, preferred_element_type=jnp.float32
    )
    grad_soft = jnp.einsum(
        "ithd,icd->ihtc", grad_heads, s["window_values"], preferred_element_type=jnp.float32
    )
    grad_scores = (
        probs * (grad_soft - jnp.sum(probs * grad_soft, axis=-1, keepdims=True))
    ).astype(low)
    grad_keys_win = jnp.einsum(
        "ihtc,ithd->icd", grad_scores, s["queries"], preferred_element_type=jnp.float32
    )
    grad_queries = jnp.einsum(
        "ihtc,icd->ithd", grad_scores, s["window_keys"], preferred_element_type=jnp.float32
    ).reshape(rows, -1, head_width)
    own_pair = return_edges(
        jnp.concatenate([grad_keys_win, grad_values_win], axis=2), hops, rows_here
    ).reshape(rows, -1)
    out["lru"] = product_tn(grad_lowrank_out, s["lowrank_mid"])
    grad_lowrank_mid = product(grad_lowrank_out, w["lru"]).astype(low)
    out["lrd"] = product_tn(s["normed"], grad_lowrank_mid)

    def query_fn(pre, gain):
        return head_path(pre, gain, cosines, sines, head_width ** (-0.5))

    def key_fn(pre, gain):
        return head_path(pre, gain, cosines, sines, 1.0)

    _, query_pull = jax.vjp(query_fn, s["q_pre"], w["qk"][0])
    _, key_pull = jax.vjp(key_fn, s["k_pre"], w["qk"][1])
    grad_q_pre, grad_q_gain = query_pull(grad_queries)
    grad_k_pre, grad_k_gain = key_pull(own_pair[:, None, :head_width])
    grad_q_pre = grad_q_pre.astype(low)
    grad_kv = jnp.concatenate([grad_k_pre, own_pair[:, head_width:]], axis=1).astype(low)
    width = grad_q_pre.shape[1] // 2
    grad_q_parts = [grad_q_pre[:, :width], grad_q_pre[:, width:]]
    out["q"] = [product_tn(s["normed"], part) for part in grad_q_parts]
    out["kv"] = product_tn(s["normed"], grad_kv)
    grad_normed = (
        product_nt(grad_lowrank_mid, w["lrd"])
        + product_nt(grad_q_parts[0], w["q"][0])
        + product_nt(grad_q_parts[1], w["q"][1])
        + product_nt(grad_kv, w["kv"])
    )
    grad_inputs, gain_zero = norm_back(s["inputs"], g[0], grad_normed)
    out["gains"] = jnp.stack([gain_zero, gain_one, gain_two, gain_three, gain_four])
    out["qk"] = jnp.stack([grad_q_gain, grad_k_gain])
    return grad_inputs + grad_first, out


BIG = ("q", "o", "gate", "up", "down")
CHAIN_ORDER = {"misc": 0, "q": 1, "o": 0, "gate": 0, "up": 1, "down": 2}
LANES = 128


def pad_columns(value, columns):
    return jnp.pad(value, ((0, 0), (0, columns - value.shape[1])))


def local(
    tokens,
    layer_inputs,
    doc_lengths,
    order,
    out_grad,
    query_weight,
    key_weight,
    value_weight,
    output_weight,
    gate_weight,
    up_weight,
    down_weight,
    lowrank_down,
    lowrank_up,
    input_gate,
    input_proj,
    norm_gains,
    qk_gains,
):
    section = lax.axis_index("section")
    block_index = lax.axis_index("seq")
    first = section == 0
    micro_count = order.shape[1]
    steps = micro_count // 2
    rows_here = tokens.shape[1]
    width = tokens.shape[2]
    rows = steps * rows_here
    hops = (WINDOW - 2) // rows_here + 1
    shard_rows = query_weight.shape[1]
    head_width = key_weight.shape[2]
    head_shard = qk_gains.shape[2]
    gain_count = norm_gains.shape[1]
    shard_count = lax.axis_size("seq") * lax.axis_size("fsdp")
    shard_index = block_index * lax.axis_size("fsdp") + lax.axis_index("fsdp")
    rank = lowrank_down.shape[2]
    extra_width = input_gate.shape[2]
    orders = stage_orders()

    def choose(one, two):
        return jnp.where(first, one, two)

    def halves(value):
        middle = value.shape[1] // 2
        return value[:, :middle], value[:, middle:]

    out_shard, down_shard = output_weight[0].T, down_weight[0].T
    proj_shard, lru_shard = input_proj[0].T, lowrank_up[0].T
    qk_flat = qk_gains[0].reshape(-1)
    qk_columns = -(-qk_flat.shape[0] // shard_rows)
    qk_block = (
        jnp.pad(qk_flat, (0, qk_columns * shard_rows - qk_flat.shape[0]))
        .reshape(qk_columns, shard_rows)
        .T
    )
    gain_block = norm_gains[0].T
    used = head_width + extra_width + rank + gain_count + qk_columns
    misc_columns = -(-used // LANES) * LANES

    def misc_half(at):
        return pad_columns(
            jnp.concatenate(
                [
                    (key_weight[0], value_weight[0])[at],
                    halves(input_gate[0])[at],
                    halves(proj_shard)[at],
                    halves(lowrank_down[0])[at],
                    halves(lru_shard)[at],
                    gain_block,
                    qk_block,
                ],
                axis=1,
            ),
            misc_columns,
        )

    shard_halves = {
        "misc": (misc_half(0), misc_half(1)),
        "q": halves(query_weight[0]),
        "o": halves(out_shard),
        "gate": halves(gate_weight[0]),
        "up": halves(up_weight[0]),
        "down": halves(down_shard),
    }
    names = ("misc",) + BIG
    sizes = [shard_halves[n][0].shape[1] for n in names]
    both = [jnp.concatenate([shard_halves[n][at] for n in names], axis=1) for at in range(2)]
    kept = choose(both[0], both[1])
    received = swap_cores(choose(both[1], both[0]))
    layer_packs = (choose(kept, received), choose(received, kept))

    def gathered(pack):
        result, start = {}, 0
        for name, size in zip(names, sizes):
            mine = gather_rows(pack[:, start : start + size], orders[CHAIN_ORDER[name]])
            result[name] = (mine, swap_cores(mine))
            start += size
        mine, other = result.pop("misc")
        low_half, high_half = choose(mine, other), choose(other, mine)
        start = head_width
        result["kv"] = jnp.concatenate([low_half[:, :start], high_half[:, :start]], axis=1)
        for name, size in (
            ("ig", extra_width // 2),
            ("ip", extra_width // 2),
            ("lrd", rank // 2),
            ("lru", rank // 2),
        ):
            result[name] = jnp.concatenate(
                [low_half[:, start : start + size], high_half[:, start : start + size]], axis=1
            )
            start += size
        result["gains"] = mine[:, start : start + gain_count].T.astype(jnp.float32)
        start += gain_count
        qk = mine[:, start : start + qk_columns].astype(jnp.float32)
        qk = qk.reshape(shard_count, shard_rows, qk_columns)
        qk = jnp.swapaxes(qk, 1, 2).reshape(shard_count, -1)[:, : 2 * head_shard]
        blocks = jnp.arange(shard_count) ^ shard_index
        qk = jnp.take(qk, blocks, axis=0).reshape(shard_count, 2, head_shard)
        result["qk"] = jnp.swapaxes(qk, 0, 1).reshape(2, -1)
        return result

    weights = [gathered(pack) for pack in layer_packs]

    column = jnp.arange(width)
    source = (shard_index ^ (column // shard_rows)) * shard_rows + column % shard_rows
    ordering = (jnp.arange(width)[:, None] == source[None, :]).astype(low)

    def to_blocks(value):
        return product(value, ordering)

    def from_blocks(value):
        return product_nt(value, ordering).astype(low)

    my_steps = [section * steps + i for i in range(steps)]
    sequence_of = [order[0][step] for step in my_steps]
    other_sequence = [order[0][(1 - section) * steps + i] for i in range(steps)]
    lengths = jnp.stack([doc_lengths[seq] for seq in sequence_of])
    ends = jnp.cumsum(lengths, axis=1)
    positions = block_index * rows_here + jnp.arange(rows_here, dtype=jnp.int32)
    key_pos = (block_index - hops) * rows_here + jnp.arange(
        (hops + 1) * rows_here, dtype=jnp.int32
    )
    passed = positions[None, :, None] >= ends[:, None, :]
    offsets = positions[None] - jnp.sum(jnp.where(passed, lengths[:, None, :], 0), axis=2)
    inverse = rope_base ** (-(jnp.arange(head_width // 2, dtype=jnp.float32) * 2.0 / head_width))
    angles = offsets.astype(jnp.float32).reshape(-1)[:, None] * inverse[None, :]
    angles = jnp.concatenate([angles, angles], axis=1)
    cosines, sines = jnp.cos(angles)[:, None, :], jnp.sin(angles)[:, None, :]
    distance = positions[:, None] - key_pos[None, :]
    near = (distance >= 0) & (distance < WINDOW) & (key_pos[None, :] >= 0)
    query_docs = doc_numbers(ends, jnp.broadcast_to(positions, (steps, rows_here)))
    key_docs = doc_numbers(ends, jnp.broadcast_to(key_pos, (steps, key_pos.shape[0])))
    pair_mask = near[None] & (query_docs[:, :, None] == key_docs[:, None, :])
    shared = (cosines, sines, pair_mask, steps, rows_here, hops)

    own_extra = layer_inputs[0]
    extra_kept = jnp.stack([own_extra[seq] for seq in sequence_of])
    extra_received = swap_cores(jnp.stack([own_extra[seq] for seq in other_sequence]))
    extras = [
        choose(extra_kept, extra_received).reshape(rows, -1).astype(jnp.float32),
        choose(extra_received, extra_kept).reshape(rows, -1).astype(jnp.float32),
    ]
    inputs = to_blocks(jnp.stack([tokens[seq] for seq in sequence_of]).reshape(rows, width))

    middle, saved_one = layer_forward(inputs, extras[0], weights[0], shared)
    middle = middle.astype(low)
    last, saved_two = layer_forward(middle.astype(jnp.float32), extras[1], weights[1], shared)
    last = last.astype(low)
    grad_last = to_blocks(
        lax.dynamic_slice_in_dim(out_grad, section * steps, steps, 0).reshape(rows, width)
    )
    grad_middle, grads_two = layer_backward(grad_last, extras[1], weights[1], saved_two, shared)
    grad_middle = grad_middle.astype(low)
    grad_tokens, grads_one = layer_backward(
        grad_middle.astype(jnp.float32), extras[0], weights[0], saved_one, shared
    )
    grad_tokens = grad_tokens.astype(low)

    def by_step(layer_one, layer_two):
        layer_one, layer_two = from_blocks(layer_one), from_blocks(layer_two)
        mine = choose(layer_one, layer_two).reshape(steps, rows_here, width)
        other = swap_cores(choose(layer_two, layer_one)).reshape(steps, rows_here, width)
        return jnp.concatenate([choose(mine, other), choose(other, mine)], axis=0)

    activations = by_step(middle, last)
    input_grads = by_step(grad_tokens, grad_middle)

    def reduced(grads):
        gains = grads["gains"].T
        qk = grads["qk"].reshape(2, shard_count, head_shard)
        qk = jnp.swapaxes(qk, 0, 1).reshape(shard_count, 2 * head_shard)
        blocks = jnp.arange(shard_count) ^ shard_index
        qk = jnp.take(qk, blocks, axis=0)
        qk = jnp.pad(qk, ((0, 0), (0, qk_columns * shard_rows - 2 * head_shard)))
        qk = jnp.swapaxes(qk.reshape(shard_count, qk_columns, shard_rows), 1, 2)
        qk = qk.reshape(width, qk_columns)

        def misc(at):
            return pad_columns(
                jnp.concatenate(
                    [
                        halves(grads["kv"])[at],
                        halves(grads["ig"])[at],
                        halves(grads["ip"])[at],
                        halves(grads["lrd"])[at],
                        halves(grads["lru"])[at],
                        gains,
                        qk,
                    ],
                    axis=1,
                ),
                misc_columns,
            ).astype(low)

        parts = {"misc": (choose(misc(0), misc(1)), choose(misc(1), misc(0)))}
        for name in BIG:
            parts[name] = grads[name]
        result = []
        for name in names:
            mine, other = parts[name]
            total = mine.astype(jnp.float32) + swap_cores(other.astype(low)).astype(jnp.float32)
            result.append(scatter_rows(total.astype(low), orders[CHAIN_ORDER[name]]))
        return jnp.concatenate(result, axis=1)

    sums_two = reduced(grads_two)
    sums_one = reduced(grads_one)
    mine = choose(sums_one, sums_two)
    other = swap_cores(choose(sums_two, sums_one))
    low_half, high_half = choose(mine, other), choose(other, mine)

    def whole_of(start, size):
        return jnp.concatenate(
            [low_half[:, start : start + size], high_half[:, start : start + size]], axis=1
        )

    start = 0
    results = {
        "key": low_half[:, :head_width],
        "value": high_half[:, :head_width],
    }
    start = head_width
    for name, size in (
        ("ig", extra_width // 2),
        ("ip", extra_width // 2),
        ("lrd", rank // 2),
        ("lru", rank // 2),
    ):
        results[name] = whole_of(start, size)
        start += size
    results["gains"] = low_half[:, start : start + gain_count].T
    start += gain_count
    qk = low_half[:, start : start + qk_columns].T.reshape(-1)[: 2 * head_shard]
    results["qk"] = qk.reshape(2, head_shard)
    start = misc_columns
    for name, size in zip(names[1:], sizes[1:]):
        results[name] = whole_of(start, size)
        start += size
    return (
        activations[None],
        input_grads[None],
        results["q"][None],
        results["key"][None],
        results["value"][None],
        results["o"].T[None],
        results["gate"][None],
        results["up"][None],
        results["down"].T[None],
        results["lrd"][None],
        results["lru"].T[None],
        results["ig"][None],
        results["ip"].T[None],
        results["gains"][None],
        results["qk"][None],
    )


def solution(mesh):
    shards = ("seq", "fsdp")
    rows_cut = P("section", shards, None)
    columns_cut = P("section", None, shards)
    steps_cut = P("section", "fsdp", "seq", None)
    in_specs = (
        P("fsdp", "seq", None),
        steps_cut,
        P("fsdp", None),
        P("fsdp", None),
        P("fsdp", "seq", None),
        rows_cut,
        rows_cut,
        rows_cut,
        columns_cut,
        rows_cut,
        rows_cut,
        columns_cut,
        rows_cut,
        columns_cut,
        rows_cut,
        columns_cut,
        columns_cut,
        columns_cut,
    )
    out_specs = (
        steps_cut,
        steps_cut,
        rows_cut,
        rows_cut,
        rows_cut,
        columns_cut,
        rows_cut,
        rows_cut,
        columns_cut,
        rows_cut,
        columns_cut,
        rows_cut,
        columns_cut,
        columns_cut,
        columns_cut,
    )
    return jax.shard_map(local, mesh=mesh, in_specs=in_specs, out_specs=out_specs, check_vma=False)
```

```python
import functools

import jax
import jax.numpy as jnp
from jax import lax
from jax.experimental import pallas as pl
from jax.experimental.pallas import tpu as pltpu
from jax.sharding import PartitionSpec as P

WINDOW = 512

epsilon = 1e-06
rope_base = 10000.0
masked_score = -1e30
low = jnp.bfloat16
wide = jnp.float32
LANES = 128
TILE = 256
GAIN_ROWS = 8
VMEM_BYTES = 48 * 2**20


def product(left, right):
    return jnp.dot(left, right, preferred_element_type=wide)


def product_nt(left, right):
    return lax.dot_general(left, right, (((1,), (1,)), ((), ())), preferred_element_type=wide)


def swap_cores(value):
    return lax.ppermute(value, "section", [(0, 1), (1, 0)])


def from_behind(value, steps):
    count = lax.axis_size("seq")
    leading, last = (max(0, -steps), min(count, count - steps))
    return lax.ppermute(value, "seq", [(source, source + steps) for source in range(leading, last)])


def index_bits():
    bits = []
    for axis in ("seq", "fsdp"):
        count = lax.axis_size(axis)
        assert count & (count - 1) == 0
        distance = count // 2
        while distance:
            bits.append((axis, distance))
            distance //= 2
    return bits


def partner_swap(value, bit):
    axis, distance = bit
    count = lax.axis_size(axis)
    return lax.ppermute(value, axis, [(i, i ^ distance) for i in range(count)])


def stage_orders():
    bits = index_bits()
    seq_places = [i for i, b in enumerate(bits) if b[0] == "seq"]
    fsdp_places = [i for i, b in enumerate(bits) if b[0] == "fsdp"]
    far, near = seq_places[:-1], seq_places[-1:]
    return {
        "near_fsdp": far + near + fsdp_places,
        "fsdp_near": far + fsdp_places + near,
        "far_last": near + fsdp_places + far,
    }


def gather_rows(shard, order):
    bits = index_bits()
    value = shard.reshape((1,) * len(bits) + shard.shape)
    for place in order:
        value = jnp.concatenate([value, partner_swap(value, bits[place])], axis=place)
    return value.reshape(-1, shard.shape[-1])


def scatter_rows(whole, order):
    bits = index_bits()
    rows = whole.shape[0] >> len(bits)
    value = whole.reshape((2,) * len(bits) + (rows, whole.shape[-1]))
    for at, place in enumerate(reversed(order)):
        kept = lax.slice_in_dim(value, 0, 1, axis=place)
        sent = lax.slice_in_dim(value, 1, 2, axis=place)
        value = kept.astype(wide) + partner_swap(sent, bits[place]).astype(wide)
        if at < len(order) - 1:
            value = value.astype(low)
    return value.reshape(rows, -1)


def run(body, grid, ins, outs, scratch=(), flops=0):
    def spec(block, index):
        if index is None:
            return pl.BlockSpec(block, lambda *at: (0,) * len(block))
        return pl.BlockSpec(block, index)

    moved = sum(a.size * a.dtype.itemsize for a, _, _ in ins)
    return pl.pallas_call(
        body,
        grid=grid,
        in_specs=[spec(block, index) for _, block, index in ins],
        out_specs=[spec(block, index) for _, _, block, index in outs],
        out_shape=[jax.ShapeDtypeStruct(shape, dtype) for shape, dtype, _, _ in outs],
        scratch_shapes=list(scratch),
        compiler_params=pltpu.CompilerParams(
            vmem_limit_bytes=VMEM_BYTES, dimension_semantics=("arbitrary",) * len(grid)
        ),
        cost_estimate=pl.CostEstimate(flops=flops, bytes_accessed=moved, transcendentals=0),
    )(*[a for a, _, _ in ins])


def rms_factor(value):
    return lax.rsqrt(jnp.mean(value * value, axis=-1, keepdims=True) + epsilon)


def rms_scale(value, gain):
    return value * rms_factor(value) * gain


def norm_back(value, gain, grad):
    factor = rms_factor(value)
    scaled = value * factor
    inner = grad * gain
    result = factor * (inner - scaled * jnp.mean(inner * scaled, axis=-1, keepdims=True))
    return result, jnp.sum(grad * scaled, axis=0, keepdims=True)


GELU_A, GELU_B = 0.7978845608028654, 0.044715


def gelu_parts(value):
    square = value * value
    turn = jnp.tanh(GELU_A * value * (1.0 + GELU_B * square))
    half = 0.5 * (1.0 + turn)
    slope = half + 0.5 * value * (1.0 - turn * turn) * GELU_A * (1.0 + 3.0 * GELU_B * square)
    return value * half, slope


def gelu(value):
    turn = jnp.tanh(GELU_A * value * (1.0 + GELU_B * value * value))
    return value * (0.5 * (1.0 + turn))


def rotate(value, cosines, sines):
    half = value.shape[1] // 2
    one, two = value[:, :half], value[:, half:]
    return jnp.concatenate([one * cosines - two * sines, two * cosines + one * sines], axis=1)


def rotate_back(value, cosines, sines):
    half = value.shape[1] // 2
    one, two = value[:, :half], value[:, half:]
    return jnp.concatenate([one * cosines + two * sines, two * cosines - one * sines], axis=1)


def add_to(ref, value, at):
    @pl.when(at == 0)
    def _():
        ref[...] = value

    @pl.when(at > 0)
    def _():
        ref[...] += value


def gain_rows(pairs, columns):
    place = lax.broadcasted_iota(jnp.int32, (GAIN_ROWS, columns), 0)
    result = jnp.zeros((GAIN_ROWS, columns), wide)
    for at, row in pairs:
        result = result + jnp.where(place == at, row, 0.0)
    return result


def row_tiles(rows):
    tile = min(rows, TILE)
    return tile, rows // tile


def by_row(i):
    return (i, 0)


def by_column(i):
    return (0, i)


def project(x, g, w, shared):
    cosines, sines, head_width, rank = (shared[k] for k in ("cos", "sin", "hd", "rank"))
    rows, width = x.shape
    tile, count = row_tiles(rows)
    q_columns = w["q_columns"]
    heads = q_columns // head_width
    slot = w["slot"]

    def body(x_r, g_r, qk_r, q1_r, q2_r, lo_r, hi_r, cos_r, sin_r, n1t, queries, kv, qpre, kpre, mid):
        value = x_r[...].astype(wide)
        normed = rms_scale(value, g_r[0:1]).astype(low)
        n1t[...] = normed.T
        cosine, sine = cos_r[...], sin_r[...]
        kp = product(normed, lo_r[:, :head_width])
        kpre[...] = kp.astype(low)
        kv[:, :head_width] = rotate(rms_scale(kp, qk_r[1:2]), cosine, sine).astype(low)
        kv[:, head_width:] = product(normed, hi_r[:, :head_width]).astype(low)
        mid[...] = product(normed, lo_r[:, slot : slot + LANES])[:, :rank].astype(low)
        for at, q_r in enumerate((q1_r, q2_r)):
            pre = product(normed, q_r[...])
            for head in range(heads):
                one = pre[:, head * head_width : (head + 1) * head_width]
                start = at * q_columns + head * head_width
                qpre[:, start : start + head_width] = one.astype(low)
                turned = rotate(rms_scale(one, qk_r[0:1]), cosine, sine) * head_width ** (-0.5)
                queries[:, start : start + head_width] = turned.astype(low)

    every = 2 * q_columns
    misc = w["lo"].shape[1]
    return run(
        body,
        (count,),
        [
            (x, (tile, width), by_row),
            (g, g.shape, None),
            (w["qk"], w["qk"].shape, None),
            (w["x"][0], (width, q_columns), None),
            (w["x"][1], (width, q_columns), None),
            (w["lo"], (width, misc), None),
            (w["hi"], (width, misc), None),
            (cosines, (tile, head_width // 2), by_row),
            (sines, (tile, head_width // 2), by_row),
        ],
        [
            ((width, rows), low, (width, tile), by_column),
            ((rows, every), low, (tile, every), by_row),
            ((rows, 2 * head_width), low, (tile, 2 * head_width), by_row),
            ((rows, every), low, (tile, every), by_row),
            ((rows, head_width), low, (tile, head_width), by_row),
            ((rows, rank), low, (tile, rank), by_row),
        ],
        flops=2 * rows * width * (every + 2 * head_width + LANES),
    )


def window_probs(query, keys, lowest, span):
    scores = product_nt(query, keys)
    place = lax.broadcasted_iota(jnp.int32, scores.shape, 1)
    newest = lax.broadcasted_iota(jnp.int32, scores.shape, 0) + span
    scores = jnp.where((place >= lowest) & (place <= newest), scores, masked_score)
    powers = jnp.exp(scores - jnp.max(scores, axis=-1, keepdims=True))
    return powers * (1.0 / jnp.sum(powers, axis=-1, keepdims=True))


def attend(queries, pieces, shared):
    lowest, head_width, steps = (shared[k] for k in ("lowest", "hd", "steps"))
    rows, every = queries.shape
    here = rows // steps
    hops = len(pieces) - 1

    def body(q_r, low_r, *rest):
        piece_refs, mixed = rest[:-1], rest[-1]
        keys = jnp.concatenate([p[:, :head_width] for p in piece_refs], axis=0)
        values = jnp.concatenate([p[:, head_width:] for p in piece_refs], axis=0)
        probs = window_probs(q_r[...], keys, low_r[...], hops * here)
        mixed[...] = product(probs.astype(low), values).astype(low)

    return run(
        body,
        (steps, every // head_width),
        [
            (queries, (here, head_width), lambda i, h: (i, h)),
            (lowest, (here, 1), lambda i, h: (i, 0)),
        ]
        + [(p, (here, 2 * head_width), lambda i, h: (i, 0)) for p in pieces],
        [((rows, every), low, (here, head_width), lambda i, h: (i, h))],
        flops=4 * rows * every * (hops + 1) * here,
    )[0]


def attention_out(x, mixed, mid, g, w, shared):
    rank, slot = shared["rank"], w["slot"]
    rows, width = x.shape
    tile, count = row_tiles(rows)
    half = w["q_columns"]

    def body(x_r, mixed_r, mid_r, g_r, o1_r, o2_r, hi_r, attn, h1, n2, n2t):
        out = product_nt(mixed_r[:, :half], o1_r[...]) + product_nt(mixed_r[:, half:], o2_r[...])
        attn[...] = out.astype(low)
        second = product_nt(mid_r[...], hi_r[:, slot : slot + LANES][:, :rank])
        total = x_r[...].astype(wide) + rms_scale(out, g_r[1:2]) + second
        h1[...] = total
        normed = rms_scale(total, g_r[2:3]).astype(low)
        n2[...] = normed
        n2t[...] = normed.T

    return run(
        body,
        (count,),
        [
            (x, (tile, width), by_row),
            (mixed, (tile, 2 * half), by_row),
            (mid, (tile, rank), by_row),
            (g, g.shape, None),
            (w["x"][0], (width, half), lambda i: (0, 1)),
            (w["x"][1], (width, half), lambda i: (0, 1)),
            (w["hi"], w["hi"].shape, None),
        ],
        [
            ((rows, width), low, (tile, width), by_row),
            ((rows, width), wide, (tile, width), by_row),
            ((rows, width), low, (tile, width), by_row),
            ((width, rows), low, (width, tile), by_column),
        ],
        flops=2 * rows * width * (2 * half + rank),
    )


def ffn(n2, gate_up, down, before):
    rows, width = n2.shape
    columns = down.shape[1]
    tile = min(TILE, columns)

    def body(n2_r, gu_r, down_r, *rest):
        saved, total = rest[-2:]
        at = pl.program_id(0)
        both = product(n2_r[...], gu_r[...])
        saved[...] = both.astype(low)
        hidden = (gelu(both[:, :tile]) * both[:, tile:]).astype(low)
        part = product_nt(hidden, down_r[...])

        @pl.when(at == 0)
        def _():
            total[...] = part + rest[0][...] if before is not None else part

        @pl.when(at > 0)
        def _():
            total[...] += part

    ins = [
        (n2, (rows, width), None),
        (gate_up, (width, 2 * tile), by_column),
        (down, (width, tile), by_column),
    ]
    if before is not None:
        ins.append((before, (rows, width), None))
    return run(
        body,
        (columns // tile,),
        ins,
        [
            ((rows, 2 * columns), low, (rows, 2 * tile), by_column),
            ((rows, width), wide, (rows, width), None),
        ],
        flops=6 * rows * width * columns,
    )


def pli_weights(lo_r, hi_r, head_width, extra_half):
    start = head_width
    gate_in = jnp.concatenate(
        [lo_r[:, start : start + extra_half], hi_r[:, start : start + extra_half]], axis=1
    )
    start += extra_half
    proj = jnp.concatenate(
        [lo_r[:, start : start + extra_half], hi_r[:, start : start + extra_half]], axis=1
    )
    return gate_in, proj


def pli(h1, ff_out, extra, g, w, shared):
    head_width = shared["hd"]
    rows, width = h1.shape
    tile, count = row_tiles(rows)
    columns = extra.shape[1]

    def body(h1_r, ff_r, extra_r, g_r, lo_r, hi_r, ff_low, h2t, pgate, mix, pout, y):
        gate_in, proj = pli_weights(lo_r, hi_r, head_width, columns // 2)
        out = ff_r[...]
        ff_low[...] = out.astype(low)
        total = h1_r[...] + rms_scale(out, g_r[3:4])
        total_low = total.astype(low)
        h2t[...] = total_low.T
        gate = product(total_low, gate_in)
        pgate[...] = gate.astype(low)
        mixed = (gelu(gate) * extra_r[...].astype(wide)).astype(low)
        mix[...] = mixed
        last = product_nt(mixed, proj)
        pout[...] = last.astype(low)
        y[...] = (total + rms_scale(last, g_r[4:5])).astype(low)

    return run(
        body,
        (count,),
        [
            (h1, (tile, width), by_row),
            (ff_out, (tile, width), by_row),
            (extra, (tile, columns), by_row),
            (g, g.shape, None),
            (w["lo"], w["lo"].shape, None),
            (w["hi"], w["hi"].shape, None),
        ],
        [
            ((rows, width), low, (tile, width), by_row),
            ((width, rows), low, (width, tile), by_column),
            ((rows, columns), low, (tile, columns), by_row),
            ((rows, columns), low, (tile, columns), by_row),
            ((rows, width), low, (tile, width), by_row),
            ((rows, width), low, (tile, width), by_row),
        ],
        flops=4 * rows * width * columns,
    )


def pli_back(grad, s, extra, g, w, shared):
    head_width = shared["hd"]
    rows, width = grad.shape
    tile, count = row_tiles(rows)
    columns = extra.shape[1]

    def body(dy_r, pout_r, mix_r, pgate_r, extra_r, ff_r, h2t_r, g_r, lo_r, hi_r, *outs):
        dh2, dff, dfft, d_in, d_proj, d_gain = outs
        at = pl.program_id(0)
        gate_in, proj = pli_weights(lo_r, hi_r, head_width, columns // 2)
        dy = dy_r[...].astype(wide)
        d_pout, gain_four = norm_back(pout_r[...].astype(wide), g_r[4:5], dy)
        d_pout = d_pout.astype(low)
        d_mix = product(d_pout, proj)
        _, slope = gelu_parts(pgate_r[...].astype(wide))
        d_gate = (d_mix * extra_r[...].astype(wide) * slope).astype(low)
        total = dy + product_nt(d_gate, gate_in)
        dh2[...] = total
        d_ff, gain_three = norm_back(ff_r[...].astype(wide), g_r[3:4], total)
        d_ff = d_ff.astype(low)
        dff[...] = d_ff
        dfft[...] = d_ff.T
        add_to(d_in, product(h2t_r[...], d_gate), at)
        add_to(d_proj, product(d_pout.T, mix_r[...]), at)
        add_to(d_gain, gain_rows([(3, gain_three), (4, gain_four)], width), at)

    return run(
        body,
        (count,),
        [
            (grad, (tile, width), by_row),
            (s["pout"], (tile, width), by_row),
            (s["mix"], (tile, columns), by_row),
            (s["pgate"], (tile, columns), by_row),
            (extra, (tile, columns), by_row),
            (s["ff"], (tile, width), by_row),
            (s["h2t"], (width, tile), by_column),
            (g, g.shape, None),
            (w["lo"], w["lo"].shape, None),
            (w["hi"], w["hi"].shape, None),
        ],
        [
            ((rows, width), wide, (tile, width), by_row),
            ((rows, width), low, (tile, width), by_row),
            ((width, rows), low, (width, tile), by_column),
            ((width, columns), wide, (width, columns), None),
            ((width, columns), wide, (width, columns), None),
            ((GAIN_ROWS, width), wide, (GAIN_ROWS, width), None),
        ],
        flops=8 * rows * width * columns,
    )


def ffn_back(dff, dfft, n2t, saved, gate_up, down, before):
    rows, width = dff.shape
    columns = down.shape[1]
    tile = min(TILE, columns)

    def body(dff_r, dfft_r, n2t_r, saved_r, gu_r, down_r, *rest):
        d_gu, d_down, total = rest[-3:]
        at = pl.program_id(0)
        up = saved_r[:, tile:].astype(wide)
        one, slope = gelu_parts(saved_r[:, :tile].astype(wide))
        d_down[...] = product(dfft_r[...], (one * up).astype(low)).astype(low)
        d_hidden = product(dff_r[...], down_r[...])
        both = jnp.concatenate(
            [(d_hidden * up * slope).astype(low), (d_hidden * one).astype(low)], axis=1
        )
        d_gu[...] = product(n2t_r[...], both).astype(low)
        part = product_nt(both, gu_r[...])

        @pl.when(at == 0)
        def _():
            total[...] = part + rest[0][...] if before is not None else part

        @pl.when(at > 0)
        def _():
            total[...] += part

    ins = [
        (dff, (rows, width), None),
        (dfft, (width, rows), None),
        (n2t, (width, rows), None),
        (saved, (rows, 2 * tile), by_column),
        (gate_up, (width, 2 * tile), by_column),
        (down, (width, tile), by_column),
    ]
    if before is not None:
        ins.append((before, (rows, width), None))
    return run(
        body,
        (columns // tile,),
        ins,
        [
            ((width, 2 * columns), low, (width, 2 * tile), by_column),
            ((width, columns), low, (width, tile), by_column),
            ((rows, width), wide, (rows, width), None),
        ],
        flops=12 * rows * width * columns,
    )


def attention_out_back(dn2, dh2, s, g, w, shared):
    rank, slot = shared["rank"], w["slot"]
    rows, width = dn2.shape
    tile, count = row_tiles(rows)
    half = w["q_columns"]

    def body(dn2_r, dh2_r, h1_r, attn_r, mixed_r, mid_r, n1t_r, g_r, o1_r, o2_r, lo_r, hi_r, *rest):
        dh1, d_mixed, d_mid, d_o1, d_o2, d_lrd, d_lru, d_gain, sum_o = rest
        at = pl.program_id(0)
        part, gain_two = norm_back(h1_r[...], g_r[2:3], dn2_r[...])
        total = part + dh2_r[...]
        dh1[...] = total
        d_attn, gain_one = norm_back(attn_r[...].astype(wide), g_r[1:2], total)
        d_attn = d_attn.astype(low)
        add_to(sum_o, product(d_attn.T, mixed_r[...]), at)
        d_mixed[:, :half] = product(d_attn, o1_r[...]).astype(low)
        d_mixed[:, half:] = product(d_attn, o2_r[...]).astype(low)
        d_lr = total.astype(low)
        d_middle = product(d_lr, hi_r[:, slot : slot + LANES])[:, :rank].astype(low)
        d_mid[...] = d_middle
        add_to(d_lru, product(d_lr.T, mid_r[...]), at)
        add_to(d_lrd, product(n1t_r[...], d_middle), at)
        add_to(d_gain, gain_rows([(1, gain_one), (2, gain_two)], width), at)

        @pl.when(at == count - 1)
        def _():
            d_o1[...] = sum_o[:, :half].astype(low)
            d_o2[...] = sum_o[:, half:].astype(low)

    return run(
        body,
        (count,),
        [
            (dn2, (tile, width), by_row),
            (dh2, (tile, width), by_row),
            (s["h1"], (tile, width), by_row),
            (s["attn"], (tile, width), by_row),
            (s["mixed"], (tile, 2 * half), by_row),
            (s["mid"], (tile, rank), by_row),
            (s["n1t"], (width, tile), by_column),
            (g, g.shape, None),
            (w["x"][0], (width, half), lambda i: (0, 1)),
            (w["x"][1], (width, half), lambda i: (0, 1)),
            (w["lo"], w["lo"].shape, None),
            (w["hi"], w["hi"].shape, None),
        ],
        [
            ((rows, width), wide, (tile, width), by_row),
            ((rows, 2 * half), low, (tile, 2 * half), by_row),
            ((rows, rank), low, (tile, rank), by_row),
            ((width, half), low, (width, half), None),
            ((width, half), low, (width, half), None),
            ((width, rank), wide, (width, rank), None),
            ((width, rank), wide, (width, rank), None),
            ((GAIN_ROWS, width), wide, (GAIN_ROWS, width), None),
        ],
        scratch=[pltpu.VMEM((width, 2 * half), wide)],
        flops=4 * rows * width * (2 * half + 2 * rank),
    )


def attend_back(d_mixed, s, pieces, w, shared):
    lowest, head_width, steps = (shared[k] for k in ("lowest", "hd", "steps"))
    rows, every = d_mixed.shape
    here = rows // steps
    hops = len(pieces) - 1
    heads = every // head_width

    def body(q_r, low_r, dm_r, qpre_r, cos_r, sin_r, qk_r, *rest):
        piece_refs, rest = rest[: hops + 1], rest[hops + 1 :]
        d_qpre, d_own, d_gain = rest[:3]
        edges, (sum_k, sum_v) = rest[3 : 3 + hops], rest[3 + hops :]
        step, head = pl.program_id(0), pl.program_id(1)
        keys = jnp.concatenate([p[:, :head_width] for p in piece_refs], axis=0)
        values = jnp.concatenate([p[:, head_width:] for p in piece_refs], axis=0)
        query, d_m = q_r[...], dm_r[...]
        probs = window_probs(query, keys, low_r[...], hops * here)
        add_to(sum_v, product(probs.astype(low).T, d_m), head)
        d_probs = product_nt(d_m, values)
        d_scores = probs * (d_probs - jnp.sum(probs * d_probs, axis=-1, keepdims=True))
        d_scores = d_scores.astype(low)
        add_to(sum_k, product(d_scores.T, query), head)
        d_query = product(d_scores, keys) * head_width ** (-0.5)
        d_pre, gain = norm_back(
            qpre_r[...].astype(wide), qk_r[0:1], rotate_back(d_query, cos_r[...], sin_r[...])
        )
        d_qpre[...] = d_pre.astype(low)
        add_to(d_gain, gain_rows([(0, gain)], head_width), step * heads + head)

        @pl.when(head == heads - 1)
        def _():
            for at in range(hops):
                part = slice(at * here, (at + 1) * here)
                edges[at][:, :head_width] = sum_k[part].astype(low)
                edges[at][:, head_width:] = sum_v[part].astype(low)
            d_own[:, :head_width] = sum_k[hops * here :]
            d_own[:, head_width:] = sum_v[hops * here :]

    both = 2 * head_width
    outs = run(
        body,
        (steps, heads),
        [
            (s["queries"], (here, head_width), lambda i, h: (i, h)),
            (lowest, (here, 1), lambda i, h: (i, 0)),
            (d_mixed, (here, head_width), lambda i, h: (i, h)),
            (s["qpre"], (here, head_width), lambda i, h: (i, h)),
            (shared["cos"], (here, head_width // 2), lambda i, h: (i, 0)),
            (shared["sin"], (here, head_width // 2), lambda i, h: (i, 0)),
            (w["qk"], w["qk"].shape, None),
        ]
        + [(p, (here, both), lambda i, h: (i, 0)) for p in pieces],
        [
            ((rows, every), low, (here, head_width), lambda i, h: (i, h)),
            ((rows, both), wide, (here, both), lambda i, h: (i, 0)),
            ((GAIN_ROWS, head_width), wide, (GAIN_ROWS, head_width), None),
        ]
        + [((rows, both), low, (here, both), lambda i, h: (i, 0)) for _ in range(hops)],
        scratch=[pltpu.VMEM(((hops + 1) * here, head_width), wide)] * 2,
        flops=10 * rows * every * (hops + 1) * here,
    )
    return outs[0], outs[1], outs[2], outs[3:]


def query_back(d_qpre, d_mid, s, w, shared):
    rank, slot = shared["rank"], w["slot"]
    rows, every = d_qpre.shape
    width = s["n1t"].shape[0]
    tile, count = row_tiles(rows)
    half = every // 2

    def body(dq_r, dmid_r, n1t_r, q1_r, q2_r, lo_r, dn1, d_q1, d_q2, sum_q):
        at = pl.program_id(0)
        value = dq_r[...]
        dn1[...] = (
            product_nt(value[:, :half], q1_r[...])
            + product_nt(value[:, half:], q2_r[...])
            + product_nt(dmid_r[...], lo_r[:, slot : slot + LANES][:, :rank])
        )
        add_to(sum_q, product(n1t_r[...], value), at)

        @pl.when(at == count - 1)
        def _():
            d_q1[...] = sum_q[:, :half].astype(low)
            d_q2[...] = sum_q[:, half:].astype(low)

    return run(
        body,
        (count,),
        [
            (d_qpre, (tile, every), by_row),
            (d_mid, (tile, rank), by_row),
            (s["n1t"], (width, tile), by_column),
            (w["x"][0], (width, half), None),
            (w["x"][1], (width, half), None),
            (w["lo"], w["lo"].shape, None),
        ],
        [
            ((rows, width), wide, (tile, width), by_row),
            ((width, half), low, (width, half), None),
            ((width, half), low, (width, half), None),
        ],
        scratch=[pltpu.VMEM((width, every), wide)],
        flops=4 * rows * width * every,
    )


def key_back(d_own, received, dn1, dh1, x, s, g, w, shared):
    head_width = shared["hd"]
    rows, width = x.shape
    tile, count = row_tiles(rows)
    both = 2 * head_width
    hops = len(received)

    def body(own_r, dn1_r, dh1_r, x_r, kpre_r, n1t_r, cos_r, sin_r, qk_r, g_r, lo_r, hi_r, *rest):
        edges, (dx, d_kv, d_gain, d_key_gain) = rest[:hops], rest[hops:]
        at = pl.program_id(0)
        total = own_r[...]
        for edge in edges:
            total = total + edge[...].astype(wide)
        d_pre, key_gain = norm_back(
            kpre_r[...].astype(wide),
            qk_r[1:2],
            rotate_back(total[:, :head_width], cos_r[...], sin_r[...]),
        )
        d_k, d_v = d_pre.astype(low), total[:, head_width:].astype(low)
        add_to(d_kv, product(n1t_r[...], jnp.concatenate([d_k, d_v], axis=1)), at)
        d_normed = (
            dn1_r[...]
            + product_nt(d_k, lo_r[:, :head_width])
            + product_nt(d_v, hi_r[:, :head_width])
        )
        part, gain_zero = norm_back(x_r[...].astype(wide), g_r[0:1], d_normed)
        dx[...] = (part + dh1_r[...]).astype(low)
        add_to(d_gain, gain_rows([(0, gain_zero)], width), at)
        add_to(d_key_gain, gain_rows([(1, key_gain)], head_width), at)

    return run(
        body,
        (count,),
        [
            (d_own, (tile, both), by_row),
            (dn1, (tile, width), by_row),
            (dh1, (tile, width), by_row),
            (x, (tile, width), by_row),
            (s["kpre"], (tile, head_width), by_row),
            (s["n1t"], (width, tile), by_column),
            (shared["cos"], (tile, head_width // 2), by_row),
            (shared["sin"], (tile, head_width // 2), by_row),
            (w["qk"], w["qk"].shape, None),
            (g, g.shape, None),
            (w["lo"], w["lo"].shape, None),
            (w["hi"], w["hi"].shape, None),
        ]
        + [(edge, (tile, both), by_row) for edge in received],
        [
            ((rows, width), low, (tile, width), by_row),
            ((width, both), wide, (width, both), None),
            ((GAIN_ROWS, width), wide, (GAIN_ROWS, width), None),
            ((GAIN_ROWS, head_width), wide, (GAIN_ROWS, head_width), None),
        ],
        flops=4 * rows * width * both,
    )


def layer_forward(x, extra, w, shared, fetch):
    g = w["gains"]
    n1t, queries, kv, qpre, kpre, mid = project(x, g, w, shared)
    pieces = fetch(kv)
    mixed = attend(queries, pieces, shared)
    attn, h1, n2, n2t = attention_out(x, mixed, mid, g, w, shared)
    saved_one, total = ffn(n2, w["y"][0], w["z"][0], None)
    saved_two, total = ffn(n2, w["y"][1], w["z"][1], total)
    ff, h2t, pgate, mix, pout, y = pli(h1, total, extra, g, w, shared)
    saved = dict(
        x=x, n1t=n1t, queries=queries, qpre=qpre, kpre=kpre, mid=mid, pieces=pieces, mixed=mixed,
        attn=attn, h1=h1, n2t=n2t, gu=(saved_one, saved_two), ff=ff, h2t=h2t, pgate=pgate, mix=mix,
        pout=pout,
    )
    return y, saved


def layer_backward(grad, extra, w, s, shared, send_back):
    g = w["gains"]
    out = {}
    dh2, dff, dfft, out["ig"], out["ip"], gains_a = pli_back(grad, s, extra, g, w, shared)
    gu_two, down_two, dn2 = ffn_back(dff, dfft, s["n2t"], s["gu"][1], w["y"][1], w["z"][1], None)
    gu_one, down_one, dn2 = ffn_back(dff, dfft, s["n2t"], s["gu"][0], w["y"][0], w["z"][0], dn2)
    out["y"], out["z"] = (gu_one, gu_two), (down_one, down_two)
    dh1, d_mixed, d_mid, o_one, o_two, out["lrd"], out["lru"], gains_b = attention_out_back(
        dn2, dh2, s, g, w, shared
    )
    out["o"] = (o_one, o_two)
    d_qpre, d_own, q_gain, edges = attend_back(d_mixed, s, s["pieces"], w, shared)
    received = send_back(edges)
    dn1, q_one, q_two = query_back(d_qpre, d_mid, s, w, shared)
    out["q"] = (q_one, q_two)
    dx, out["kv"], gains_c, k_gain = key_back(d_own, received, dn1, dh1, s["x"], s, g, w, shared)
    out["gains"] = gains_a + gains_b + gains_c
    out["qk"] = (q_gain + k_gain)[:2]
    return dx, out


ORDER_OF = {"x": "near_fsdp", "y": "fsdp_near", "z": "far_last"}
SUM_ORDER_OF = {
    "y": "fsdp_near",
    "z": "far_last",
    "o": "near_fsdp",
    "q": "near_fsdp",
    "misc": "fsdp_near",
}


def pad_columns(value, columns):
    return jnp.pad(value, ((0, 0), (0, columns - value.shape[1])))


def halves(value):
    middle = value.shape[1] // 2
    return value[:, :middle], value[:, middle:]


def interleave(one, two):
    tile = min(TILE, one.shape[1])
    parts = []
    for start in range(0, one.shape[1], tile):
        parts += [one[:, start : start + tile], two[:, start : start + tile]]
    return jnp.concatenate(parts, axis=1)


def separate(value):
    columns = value.shape[1] // 2
    tile = min(TILE, columns)
    starts = range(0, 2 * columns, 2 * tile)
    one = jnp.concatenate([value[:, s : s + tile] for s in starts], axis=1)
    two = jnp.concatenate([value[:, s + tile : s + 2 * tile] for s in starts], axis=1)
    return one, two


def local(
    tokens,
    layer_inputs,
    doc_lengths,
    order,
    out_grad,
    query_weight,
    key_weight,
    value_weight,
    output_weight,
    gate_weight,
    up_weight,
    down_weight,
    lowrank_down,
    lowrank_up,
    input_gate,
    input_proj,
    norm_gains,
    qk_gains,
):
    section = lax.axis_index("section")
    block_index = lax.axis_index("seq")
    first = section == 0
    micro_count = order.shape[1]
    steps = micro_count // 2
    rows_here = tokens.shape[1]
    width = tokens.shape[2]
    rows = steps * rows_here
    hops = (WINDOW - 2) // rows_here + 1
    shard_rows = query_weight.shape[1]
    head_width = key_weight.shape[2]
    head_shard = qk_gains.shape[2]
    gain_count = norm_gains.shape[1]
    shard_count = lax.axis_size("seq") * lax.axis_size("fsdp")
    shard_index = block_index * lax.axis_size("fsdp") + lax.axis_index("fsdp")
    rank = lowrank_down.shape[2]
    extra_half = input_gate.shape[2] // 2
    q_columns = query_weight.shape[2] // 2
    slot = head_width + 2 * extra_half
    orders = stage_orders()
    assert 2 * head_shard <= shard_rows and gain_count < GAIN_ROWS
    assert rank + GAIN_ROWS <= LANES

    def choose(one, two):
        return jnp.where(first, one, two)

    qk_column = jnp.pad(qk_gains[0].reshape(1, -1), ((0, 0), (0, shard_rows - 2 * head_shard)))
    gain_block = jnp.concatenate([norm_gains[0], qk_column], axis=0).T
    q_halves, o_halves = halves(query_weight[0]), halves(output_weight[0].T)
    in_halves, proj_halves = halves(input_gate[0]), halves(input_proj[0].T)
    kv_halves = (key_weight[0], value_weight[0])
    rank_halves = (lowrank_down[0], lowrank_up[0].T)
    gate_halves, up_halves = halves(gate_weight[0]), halves(up_weight[0])
    down_halves = halves(down_weight[0].T)

    def pack(at):
        last = pad_columns(jnp.concatenate([rank_halves[at], gain_block], axis=1), LANES)
        return jnp.concatenate(
            [
                q_halves[at],
                o_halves[at],
                kv_halves[at],
                in_halves[at],
                proj_halves[at],
                last,
                interleave(gate_halves[at], up_halves[at]),
                down_halves[at],
            ],
            axis=1,
        )

    packs = [pack(at) for at in range(2)]
    x_columns = 2 * q_columns + slot + LANES
    ff_half = down_halves[0].shape[1]
    kept = choose(packs[0], packs[1])
    received = swap_cores(choose(packs[1], packs[0]))
    layer_packs = (choose(kept, received), choose(received, kept))

    place = jnp.arange(2 * shard_count * head_shard)
    half_at, head_at = place // (shard_count * head_shard), place % (shard_count * head_shard)
    qk_source = (
        ((head_at // head_shard) ^ shard_index) * shard_rows
        + half_at * head_shard
        + head_at % head_shard
    )
    qk_ordering = (jnp.arange(width)[:, None] == qk_source[None, :]).astype(low)

    def gathered(packed):
        result = {"q_columns": q_columns, "slot": slot}
        bounds = {
            "x": (0, x_columns),
            "y": (x_columns, x_columns + 2 * ff_half),
            "z": (x_columns + 2 * ff_half, x_columns + 3 * ff_half),
        }
        for name, (start, stop) in bounds.items():
            mine = gather_rows(packed[:, start:stop], orders[ORDER_OF[name]])
            result[name] = (mine, swap_cores(mine))
        mine, other = (part[:, 2 * q_columns :] for part in result["x"])
        result["lo"], result["hi"] = choose(mine, other), choose(other, mine)
        gains = mine[:, slot + rank : slot + rank + GAIN_ROWS].T
        result["gains"] = gains.astype(wide)
        qk = product(gains, qk_ordering)[gain_count]
        result["qk"] = qk.reshape(2, -1)
        return result

    weights = [gathered(packed) for packed in layer_packs]

    column = jnp.arange(width)
    source = (shard_index ^ (column // shard_rows)) * shard_rows + column % shard_rows
    ordering = (jnp.arange(width)[:, None] == source[None, :]).astype(low)

    def to_blocks(value):
        return product(value, ordering).astype(low)

    def from_blocks(value):
        return product_nt(value, ordering).astype(low)

    sequence_of = [order[0][section * steps + i] for i in range(steps)]
    other_sequence = [order[0][(1 - section) * steps + i] for i in range(steps)]
    lengths = jnp.stack([doc_lengths[seq] for seq in sequence_of])
    ends = jnp.cumsum(lengths, axis=1)
    positions = block_index * rows_here + jnp.arange(rows_here, dtype=jnp.int32)
    passed = positions[None, :, None] >= ends[:, None, :]
    doc_start = jnp.sum(jnp.where(passed, lengths[:, None, :], 0), axis=2)
    offsets = positions[None] - doc_start
    inverse = rope_base ** (-(jnp.arange(head_width // 2, dtype=wide) * 2.0 / head_width))
    angles = offsets.astype(wide).reshape(-1)[:, None] * inverse[None, :]
    lowest = jnp.maximum(doc_start, positions[None] - (WINDOW - 1))
    lowest = lowest - (block_index - hops) * rows_here
    shared = {
        "cos": jnp.cos(angles),
        "sin": jnp.sin(angles),
        "lowest": lowest.reshape(-1, 1),
        "hd": head_width,
        "rank": rank,
        "steps": steps,
    }

    own_extra = layer_inputs[0]
    extra_kept = jnp.stack([own_extra[seq] for seq in sequence_of]).reshape(rows, -1)
    extra_received = swap_cores(jnp.stack([own_extra[seq] for seq in other_sequence])).reshape(
        rows, -1
    )
    extras = [choose(extra_kept, extra_received), choose(extra_received, extra_kept)]
    inputs = to_blocks(jnp.stack([tokens[seq] for seq in sequence_of]).reshape(rows, width))
    grad_last = to_blocks(
        lax.dynamic_slice_in_dim(out_grad, section * steps, steps, 0).reshape(rows, width)
    )

    def fetch(kv):
        return [from_behind(kv, distance) for distance in range(hops, 0, -1)] + [kv]

    def send_back(edges):
        return [from_behind(edge, at - hops) for at, edge in enumerate(edges)]

    middle, saved_one = layer_forward(inputs, extras[0], weights[0], shared, fetch)
    last, saved_two = layer_forward(middle, extras[1], weights[1], shared, fetch)
    grad_middle, grads_two = layer_backward(
        grad_last, extras[1], weights[1], saved_two, shared, send_back
    )
    grad_tokens, grads_one = layer_backward(
        grad_middle, extras[0], weights[0], saved_one, shared, send_back
    )

    def by_step(layer_one, layer_two):
        layer_one, layer_two = from_blocks(layer_one), from_blocks(layer_two)
        mine = choose(layer_one, layer_two).reshape(steps, rows_here, width)
        other = swap_cores(choose(layer_two, layer_one)).reshape(steps, rows_here, width)
        return jnp.concatenate([choose(mine, other), choose(other, mine)], axis=0)

    activations = by_step(middle, last)
    input_grads = by_step(grad_tokens, grad_middle)

    def reduced(grads):
        qk = product_nt(grads["qk"].reshape(1, -1).astype(low), qk_ordering)
        row = jnp.arange(GAIN_ROWS)[:, None]
        gains = jnp.where(row == gain_count, qk, grads["gains"]).T.astype(low)

        def misc(at):
            last = jnp.concatenate([grads[("lrd", "lru")[at]].astype(low), gains], axis=1)
            return jnp.concatenate(
                [
                    halves(grads["kv"])[at].astype(low),
                    halves(grads["ig"])[at].astype(low),
                    halves(grads["ip"])[at].astype(low),
                    pad_columns(last, LANES),
                ],
                axis=1,
            )

        lo, hi = misc(0), misc(1)
        parts = {"misc": (choose(lo, hi), choose(hi, lo))}
        for name in ("q", "o", "y", "z"):
            parts[name] = grads[name]
        result = {}
        for name in ("z", "y", "o", "q", "misc"):
            mine, other = parts[name]
            total = mine.astype(wide) + swap_cores(other).astype(wide)
            result[name] = scatter_rows(total.astype(low), orders[SUM_ORDER_OF[name]])
        return jnp.concatenate([result[n] for n in ("q", "o", "misc", "y", "z")], axis=1)

    sums_two = reduced(grads_two)
    sums_one = reduced(grads_one)
    mine = choose(sums_one, sums_two)
    other = swap_cores(choose(sums_two, sums_one))
    low_half, high_half = choose(mine, other), choose(other, mine)

    def whole_of(start, size):
        return jnp.concatenate(
            [low_half[:, start : start + size], high_half[:, start : start + size]], axis=1
        )

    grad_query = whole_of(0, q_columns)
    grad_out = whole_of(q_columns, q_columns).T
    start = 2 * q_columns
    grad_key = low_half[:, start : start + head_width]
    grad_value = high_half[:, start : start + head_width]
    start += head_width
    grad_in = whole_of(start, extra_half)
    start += extra_half
    grad_proj = whole_of(start, extra_half).T
    start += extra_half
    grad_lrd = low_half[:, start : start + rank]
    grad_lru = high_half[:, start : start + rank].T
    gains = low_half[:, start + rank : start + rank + GAIN_ROWS].T
    grad_gains = gains[:gain_count]
    grad_qk = gains[gain_count, : 2 * head_shard].reshape(2, head_shard)
    start += LANES
    gates_ups = [separate(half[:, start : start + 2 * ff_half]) for half in (low_half, high_half)]
    grad_gate = jnp.concatenate([gates_ups[0][0], gates_ups[1][0]], axis=1)
    grad_up = jnp.concatenate([gates_ups[0][1], gates_ups[1][1]], axis=1)
    start += 2 * ff_half
    grad_down = whole_of(start, ff_half).T
    return tuple(
        value[None]
        for value in (
            activations,
            input_grads,
            grad_query,
            grad_key,
            grad_value,
            grad_out,
            grad_gate,
            grad_up,
            grad_down,
            grad_lrd,
            grad_lru,
            grad_in,
            grad_proj,
            grad_gains,
            grad_qk,
        )
    )


def solution(mesh):
    shards = ("seq", "fsdp")
    rows_cut = P("section", shards, None)
    columns_cut = P("section", None, shards)
    steps_cut = P("section", "fsdp", "seq", None)
    in_specs = (
        P("fsdp", "seq", None),
        steps_cut,
        P("fsdp", None),
        P("fsdp", None),
        P("fsdp", "seq", None),
        rows_cut,
        rows_cut,
        rows_cut,
        columns_cut,
        rows_cut,
        rows_cut,
        columns_cut,
        rows_cut,
        columns_cut,
        rows_cut,
        columns_cut,
        columns_cut,
        columns_cut,
    )
    out_specs = (
        steps_cut,
        steps_cut,
        rows_cut,
        rows_cut,
        rows_cut,
        columns_cut,
        rows_cut,
        rows_cut,
        columns_cut,
        rows_cut,
        columns_cut,
        rows_cut,
        columns_cut,
        columns_cut,
        columns_cut,
    )
    return jax.shard_map(local, mesh=mesh, in_specs=in_specs, out_specs=out_specs, check_vma=False)
```

```python
import functools
import math

import jax
import jax.numpy as jnp
from jax import lax
from jax.experimental import pallas as pl
from jax.experimental.pallas import tpu as pltpu
from jax.sharding import PartitionSpec as P

WINDOW = 512

epsilon = 1e-06
rope_base = 10000.0
masked_score = -1e30
low = jnp.bfloat16
wide = jnp.float32
LANES = 128
TILE = 256
GAIN_ROWS = 8
VMEM_BYTES = 48 * 2**20


def product(left, right):
    return jnp.dot(left, right, preferred_element_type=wide)


def product_nt(left, right):
    return lax.dot_general(left, right, (((1,), (1,)), ((), ())), preferred_element_type=wide)


def swap_cores(value):
    return lax.ppermute(value, "section", [(0, 1), (1, 0)])


def from_behind(value, steps):
    count = lax.axis_size("seq")
    leading, last = (max(0, -steps), min(count, count - steps))
    return lax.ppermute(value, "seq", [(source, source + steps) for source in range(leading, last)])


def index_bits():
    bits = []
    for axis in ("seq", "fsdp"):
        count = lax.axis_size(axis)
        assert count & (count - 1) == 0
        distance = count // 2
        while distance:
            bits.append((axis, distance))
            distance //= 2
    return bits


def partner_swap(value, bit):
    axis, distance = bit
    count = lax.axis_size(axis)
    return lax.ppermute(value, axis, [(i, i ^ distance) for i in range(count)])


class Line:
    def __init__(self):
        self.last = None

    def wait(self, value):
        if self.last is None:
            return value
        value, _ = lax.optimization_barrier((value, self.last))
        return value

    def done(self, value):
        self.last = value
        return value


class Links:
    def __init__(self):
        self.bits = index_bits()
        seq = [i for i, b in enumerate(self.bits) if b[0] == "seq"]
        fsdp = [i for i, b in enumerate(self.bits) if b[0] == "fsdp"]
        self.far, self.near = seq[:-1], {"one": seq[-1:] + fsdp, "two": fsdp + seq[-1:]}
        count, low_count = lax.axis_size("seq"), min(2, lax.axis_size("seq"))
        self.groups = [list(range(at, count, low_count)) for at in range(low_count)]

    def high(self, place):
        axis, distance = self.bits[place]
        return (lax.axis_index(axis) // distance) % 2 == 1

    def swap(self, value, place):
        return partner_swap(value, self.bits[place])


class Gather:
    def __init__(self, line, links, value, order=None):
        self.line, self.links, self.columns = line, links, value.shape[-1]
        form = tuple(2 if order and at in links.far else 1 for at in range(len(links.bits)))
        rows = value.shape[0] // math.prod(form)
        self.value = value.reshape(form + (rows, self.columns))
        self.order = list(links.near[order] if order else links.far)
        self.send()

    def send(self):
        self.place = self.order.pop(0)
        self.coming = self.links.swap(self.value, self.place)

    def joined(self):
        mine, other = self.value, self.line.wait(self.coming)
        straight = jnp.concatenate([mine, other], axis=self.place)
        if self.place not in self.links.far:
            return straight
        turned = jnp.concatenate([other, mine], axis=self.place)
        return jnp.where(self.links.high(self.place), turned, straight)

    def step(self):
        if self.order:
            self.value = self.line.done(self.joined())
            self.send()


def finish(*gathers):
    for gather in gathers:
        while gather.order:
            gather.step()
    parts = [c.joined().reshape(-1, c.columns) for c in gathers]
    return gathers[0].line.done(parts[0] if len(parts) == 1 else jnp.concatenate(parts, axis=1))


class Sum:
    def __init__(self, line, links, mine, received, order, with_far):
        self.line, self.links = line, links
        self.order = links.near[order][::-1] + (links.far[::-1] if with_far else [])
        self.rows = mine[0].shape[0] >> len(links.bits)
        received = [line.wait(value) for value in received]
        place = self.order[0]

        def part(value, at):
            value = value.reshape((2,) * len(links.bits) + (self.rows, value.shape[-1]))
            return lax.slice_in_dim(value, at, at + 1, axis=place).astype(wide)

        def side(at):
            both = [part(one, at) + part(two, at) for one, two in zip(mine, received)]
            return both[0] if len(both) == 1 else jnp.concatenate(both, axis=-1)

        self.kept = side(0)
        self.send(line.done(side(1).astype(low)))

    def send(self, value):
        self.coming = self.links.swap(value, self.order.pop(0))

    def total(self):
        return self.kept + self.line.wait(self.coming).astype(wide)

    def step(self):
        if not self.order:
            return
        value = self.line.done(self.total().astype(low))
        place = self.order[0]
        kept = lax.slice_in_dim(value, 0, 1, axis=place)
        sent = lax.slice_in_dim(value, 1, 2, axis=place)
        if place in self.links.far:
            high = self.links.high(place)
            kept, sent = jnp.where(high, sent, kept), jnp.where(high, kept, sent)
        self.kept = kept.astype(wide)
        self.send(sent)

    def result(self):
        while self.order:
            self.step()
        value = self.total()
        return value.reshape(-1, value.shape[-1])


def run(body, grid, ins, outs, scratch=(), flops=0):
    def spec(block, index):
        if index is None:
            return pl.BlockSpec(block, lambda *at: (0,) * len(block))
        return pl.BlockSpec(block, index)

    moved = sum(a.size * a.dtype.itemsize for a, _, _ in ins)
    return pl.pallas_call(
        body,
        grid=grid,
        in_specs=[spec(block, index) for _, block, index in ins],
        out_specs=[spec(block, index) for _, _, block, index in outs],
        out_shape=[jax.ShapeDtypeStruct(shape, dtype) for shape, dtype, _, _ in outs],
        scratch_shapes=list(scratch),
        compiler_params=pltpu.CompilerParams(
            vmem_limit_bytes=VMEM_BYTES, dimension_semantics=("arbitrary",) * len(grid)
        ),
        cost_estimate=pl.CostEstimate(flops=flops, bytes_accessed=moved, transcendentals=0),
    )(*[a for a, _, _ in ins])


def rms_factor(value):
    return lax.rsqrt(jnp.mean(value * value, axis=-1, keepdims=True) + epsilon)


def rms_scale(value, gain):
    return value * rms_factor(value) * gain


def norm_back(value, gain, grad):
    factor = rms_factor(value)
    scaled = value * factor
    inner = grad * gain
    result = factor * (inner - scaled * jnp.mean(inner * scaled, axis=-1, keepdims=True))
    return result, jnp.sum(grad * scaled, axis=0, keepdims=True)


GELU_A, GELU_B = 0.7978845608028654, 0.044715


def gelu_parts(value):
    square = value * value
    turn = jnp.tanh(GELU_A * value * (1.0 + GELU_B * square))
    half = 0.5 * (1.0 + turn)
    slope = half + 0.5 * value * (1.0 - turn * turn) * GELU_A * (1.0 + 3.0 * GELU_B * square)
    return value * half, slope


def gelu(value):
    turn = jnp.tanh(GELU_A * value * (1.0 + GELU_B * value * value))
    return value * (0.5 * (1.0 + turn))


def rotate(value, cosines, sines):
    half = value.shape[1] // 2
    one, two = value[:, :half], value[:, half:]
    return jnp.concatenate([one * cosines - two * sines, two * cosines + one * sines], axis=1)


def rotate_back(value, cosines, sines):
    half = value.shape[1] // 2
    one, two = value[:, :half], value[:, half:]
    return jnp.concatenate([one * cosines + two * sines, two * cosines - one * sines], axis=1)


def add_to(ref, value, at):
    @pl.when(at == 0)
    def _():
        ref[...] = value

    @pl.when(at > 0)
    def _():
        ref[...] += value


def gain_rows(pairs, columns):
    place = lax.broadcasted_iota(jnp.int32, (GAIN_ROWS, columns), 0)
    result = jnp.zeros((GAIN_ROWS, columns), wide)
    for at, row in pairs:
        result = result + jnp.where(place == at, row, 0.0)
    return result


def row_tiles(rows):
    tile = min(rows, TILE)
    return tile, rows // tile


def by_row(i):
    return (i, 0)


def by_column(i):
    return (0, i)


def turn_spec(w):
    return [] if w["turn"] is None else [(w["turn"], w["turn"].shape, None)]


def across(value, turn):
    if not turn:
        return value.T
    return product_nt(turn[0][...], value).astype(low)


def project(x, g, w, shared):
    cosines, sines, head_width, rank = (shared[k] for k in ("cos", "sin", "hd", "rank"))
    rows, width = x.shape
    tile, count = row_tiles(rows)
    q_columns = w["q_columns"]
    heads = q_columns // head_width
    slot = w["slot"]
    kv_at = slot - head_width

    def body(x_r, g_r, qk_r, q1_r, q2_r, lo_r, hi_r, cos_r, sin_r, *rest):
        turn, (n1t, queries, kv, qpre, kpre, mid) = rest[:-6], rest[-6:]
        value = x_r[...].astype(wide)
        normed = rms_scale(value, g_r[0:1]).astype(low)
        n1t[...] = across(normed, turn)
        cosine, sine = cos_r[...], sin_r[...]
        kp = product(normed, lo_r[:, kv_at : kv_at + head_width])
        kpre[...] = kp.astype(low)
        kv[:, :head_width] = rotate(rms_scale(kp, qk_r[1:2]), cosine, sine).astype(low)
        values = product(normed, hi_r[:, kv_at : kv_at + head_width])
        kv[:, head_width:] = values.astype(low)
        mid[...] = product(normed, lo_r[:, slot : slot + LANES])[:, :rank].astype(low)
        for at, q_r in enumerate((q1_r, q2_r)):
            pre = product(normed, q_r[...])
            for head in range(heads):
                one = pre[:, head * head_width : (head + 1) * head_width]
                start = at * q_columns + head * head_width
                qpre[:, start : start + head_width] = one.astype(low)
                turned = rotate(rms_scale(one, qk_r[0:1]), cosine, sine) * head_width ** (-0.5)
                queries[:, start : start + head_width] = turned.astype(low)

    every = 2 * q_columns
    misc = w["lo"].shape[1]
    return run(
        body,
        (count,),
        [
            (x, (tile, width), by_row),
            (g, g.shape, None),
            (w["qk"], w["qk"].shape, None),
            (w["qo"][0], (width, q_columns), lambda i: (0, w["q_at"])),
            (w["qo"][1], (width, q_columns), lambda i: (0, w["q_at"])),
            (w["lo"], (width, misc), None),
            (w["hi"], (width, misc), None),
            (cosines, (tile, head_width // 2), by_row),
            (sines, (tile, head_width // 2), by_row),
            *turn_spec(w),
        ],
        [
            ((width, rows), low, (width, tile), by_column),
            ((rows, every), low, (tile, every), by_row),
            ((rows, 2 * head_width), low, (tile, 2 * head_width), by_row),
            ((rows, every), low, (tile, every), by_row),
            ((rows, head_width), low, (tile, head_width), by_row),
            ((rows, rank), low, (tile, rank), by_row),
        ],
        flops=2 * rows * width * (every + 2 * head_width + LANES),
    )


def window_probs(query, keys, lowest, span):
    scores = product_nt(query, keys)
    place = lax.broadcasted_iota(jnp.int32, scores.shape, 1)
    newest = lax.broadcasted_iota(jnp.int32, scores.shape, 0) + span
    scores = jnp.where((place >= lowest) & (place <= newest), scores, masked_score)
    powers = jnp.exp(scores - jnp.max(scores, axis=-1, keepdims=True))
    return powers * (1.0 / jnp.sum(powers, axis=-1, keepdims=True))


def attend(queries, pieces, shared):
    lowest, head_width, steps = (shared[k] for k in ("lowest", "hd", "steps"))
    rows, every = queries.shape
    here = rows // steps
    hops = len(pieces) - 1

    def body(q_r, low_r, *rest):
        piece_refs, mixed = rest[:-1], rest[-1]
        keys = jnp.concatenate([p[:, :head_width] for p in piece_refs], axis=0)
        values = jnp.concatenate([p[:, head_width:] for p in piece_refs], axis=0)
        probs = window_probs(q_r[...], keys, low_r[...], hops * here)
        mixed[...] = product(probs.astype(low), values).astype(low)

    return run(
        body,
        (steps, every // head_width),
        [
            (queries, (here, head_width), lambda i, h: (i, h)),
            (lowest, (here, 1), lambda i, h: (i, 0)),
        ]
        + [(p, (here, 2 * head_width), lambda i, h: (i, 0)) for p in pieces],
        [((rows, every), low, (here, head_width), lambda i, h: (i, h))],
        flops=4 * rows * every * (hops + 1) * here,
    )[0]


def attention_out(x, mixed, mid, g, w, shared):
    rank, slot = shared["rank"], w["slot"]
    rows, width = x.shape
    tile, count = row_tiles(rows)
    half = w["q_columns"]

    def body(x_r, mixed_r, mid_r, g_r, o1_r, o2_r, hi_r, *rest):
        turn, (attn, h1, n2, n2t) = rest[:-4], rest[-4:]
        out = product_nt(mixed_r[:, :half], o1_r[...]) + product_nt(mixed_r[:, half:], o2_r[...])
        attn[...] = out.astype(low)
        second = product_nt(mid_r[...], hi_r[:, slot : slot + LANES][:, :rank])
        total = x_r[...].astype(wide) + rms_scale(out, g_r[1:2]) + second
        h1[...] = total
        normed = rms_scale(total, g_r[2:3]).astype(low)
        n2[...] = normed
        n2t[...] = across(normed, turn)

    return run(
        body,
        (count,),
        [
            (x, (tile, width), by_row),
            (mixed, (tile, 2 * half), by_row),
            (mid, (tile, rank), by_row),
            (g, g.shape, None),
            (w["qo"][0], (width, half), lambda i: (0, w["q_at"] + 1)),
            (w["qo"][1], (width, half), lambda i: (0, w["q_at"] + 1)),
            (w["hi"], w["hi"].shape, None),
            *turn_spec(w),
        ],
        [
            ((rows, width), low, (tile, width), by_row),
            ((rows, width), wide, (tile, width), by_row),
            ((rows, width), low, (tile, width), by_row),
            ((width, rows), low, (width, tile), by_column),
        ],
        flops=2 * rows * width * (2 * half + rank),
    )


def ffn(n2, weights, columns, before):
    rows, width = n2.shape
    tile = min(TILE, columns)

    def body(n2_r, w_r, *rest):
        saved, total = rest[-2:]
        at = pl.program_id(0)
        both = product(n2_r[...], w_r[:, : 2 * tile])
        saved[...] = both.astype(low)
        hidden = (gelu(both[:, :tile]) * both[:, tile:]).astype(low)
        part = product_nt(hidden, w_r[:, 2 * tile :])

        @pl.when(at == 0)
        def _():
            total[...] = part + rest[0][...] if before is not None else part

        @pl.when(at > 0)
        def _():
            total[...] += part

    ins = [(n2, (rows, width), None), (weights, (width, 3 * tile), by_column)]
    if before is not None:
        ins.append((before, (rows, width), None))
    return run(
        body,
        (columns // tile,),
        ins,
        [
            ((rows, 2 * columns), low, (rows, 2 * tile), by_column),
            ((rows, width), wide, (rows, width), None),
        ],
        flops=6 * rows * width * columns,
    )


def pli_weights(lo_r, hi_r, extra_half):
    start = 0
    gate_in = jnp.concatenate(
        [lo_r[:, start : start + extra_half], hi_r[:, start : start + extra_half]], axis=1
    )
    start += extra_half
    proj = jnp.concatenate(
        [lo_r[:, start : start + extra_half], hi_r[:, start : start + extra_half]], axis=1
    )
    return gate_in, proj


def pli(h1, ff_out, extra, g, w, shared):
    rows, width = h1.shape
    tile, count = row_tiles(rows)
    columns = extra.shape[1]

    def body(h1_r, ff_r, extra_r, g_r, lo_r, hi_r, *rest):
        turn, (ff_low, h2t, pgate, mix, pout, y) = rest[:-6], rest[-6:]
        gate_in, proj = pli_weights(lo_r, hi_r, columns // 2)
        out = ff_r[...]
        ff_low[...] = out.astype(low)
        total = h1_r[...] + rms_scale(out, g_r[3:4])
        total_low = total.astype(low)
        h2t[...] = across(total_low, turn)
        gate = product(total_low, gate_in)
        pgate[...] = gate.astype(low)
        mixed = (gelu(gate) * extra_r[...].astype(wide)).astype(low)
        mix[...] = mixed
        last = product_nt(mixed, proj)
        pout[...] = last.astype(low)
        y[...] = (total + rms_scale(last, g_r[4:5])).astype(low)

    return run(
        body,
        (count,),
        [
            (h1, (tile, width), by_row),
            (ff_out, (tile, width), by_row),
            (extra, (tile, columns), by_row),
            (g, g.shape, None),
            (w["lo"], w["lo"].shape, None),
            (w["hi"], w["hi"].shape, None),
            *turn_spec(w),
        ],
        [
            ((rows, width), low, (tile, width), by_row),
            ((width, rows), low, (width, tile), by_column),
            ((rows, columns), low, (tile, columns), by_row),
            ((rows, columns), low, (tile, columns), by_row),
            ((rows, width), low, (tile, width), by_row),
            ((rows, width), low, (tile, width), by_row),
        ],
        flops=4 * rows * width * columns,
    )


def pli_back(grad, s, extra, g, w, shared):
    rows, width = grad.shape
    tile, count = row_tiles(rows)
    columns = extra.shape[1]

    def body(dy_r, pout_r, mix_r, pgate_r, extra_r, ff_r, h2t_r, g_r, lo_r, hi_r, *outs):
        turn, (dh2, dff, dfft, d_in, d_proj, d_gain) = outs[:-6], outs[-6:]
        at = pl.program_id(0)
        gate_in, proj = pli_weights(lo_r, hi_r, columns // 2)
        dy = dy_r[...].astype(wide)
        d_pout, gain_four = norm_back(pout_r[...].astype(wide), g_r[4:5], dy)
        d_pout = d_pout.astype(low)
        d_mix = product(d_pout, proj)
        _, slope = gelu_parts(pgate_r[...].astype(wide))
        d_gate = (d_mix * extra_r[...].astype(wide) * slope).astype(low)
        total = dy + product_nt(d_gate, gate_in)
        dh2[...] = total
        d_ff, gain_three = norm_back(ff_r[...].astype(wide), g_r[3:4], total)
        d_ff = d_ff.astype(low)
        dff[...] = d_ff
        dfft[...] = across(d_ff, turn)
        add_to(d_in, product(h2t_r[...], d_gate), at)
        add_to(d_proj, product(across(d_pout, turn), mix_r[...]), at)
        add_to(d_gain, gain_rows([(3, gain_three), (4, gain_four)], width), at)

    return run(
        body,
        (count,),
        [
            (grad, (tile, width), by_row),
            (s["pout"], (tile, width), by_row),
            (s["mix"], (tile, columns), by_row),
            (s["pgate"], (tile, columns), by_row),
            (extra, (tile, columns), by_row),
            (s["ff"], (tile, width), by_row),
            (s["h2t"], (width, tile), by_column),
            (g, g.shape, None),
            (w["lo"], w["lo"].shape, None),
            (w["hi"], w["hi"].shape, None),
            *turn_spec(w),
        ],
        [
            ((rows, width), wide, (tile, width), by_row),
            ((rows, width), low, (tile, width), by_row),
            ((width, rows), low, (width, tile), by_column),
            ((width, columns), wide, (width, columns), None),
            ((width, columns), wide, (width, columns), None),
            ((GAIN_ROWS, width), wide, (GAIN_ROWS, width), None),
        ],
        flops=8 * rows * width * columns,
    )


def ffn_back(dff, dfft, n2t, saved, weights, before):
    rows, width = dff.shape
    columns = saved.shape[1] // 2
    tile = min(TILE, columns)

    def body(dff_r, dfft_r, n2t_r, saved_r, w_r, *rest):
        d_w, total = rest[-2:]
        at = pl.program_id(0)
        up = saved_r[:, tile:].astype(wide)
        one, slope = gelu_parts(saved_r[:, :tile].astype(wide))
        d_w[:, 2 * tile :] = product(dfft_r[...], (one * up).astype(low)).astype(low)
        d_hidden = product(dff_r[...], w_r[:, 2 * tile :])
        both = jnp.concatenate(
            [(d_hidden * up * slope).astype(low), (d_hidden * one).astype(low)], axis=1
        )
        d_w[:, : 2 * tile] = product(n2t_r[...], both).astype(low)
        part = product_nt(both, w_r[:, : 2 * tile])

        @pl.when(at == 0)
        def _():
            total[...] = part + rest[0][...] if before is not None else part

        @pl.when(at > 0)
        def _():
            total[...] += part

    ins = [
        (dff, (rows, width), None),
        (dfft, (width, rows), None),
        (n2t, (width, rows), None),
        (saved, (rows, 2 * tile), by_column),
        (weights, (width, 3 * tile), by_column),
    ]
    if before is not None:
        ins.append((before, (rows, width), None))
    return run(
        body,
        (columns // tile,),
        ins,
        [
            ((width, 3 * columns), low, (width, 3 * tile), by_column),
            ((rows, width), wide, (rows, width), None),
        ],
        flops=12 * rows * width * columns,
    )


def attention_out_back(dn2, dh2, s, g, w, shared):
    rank, slot = shared["rank"], w["slot"]
    rows, width = dn2.shape
    tile, count = row_tiles(rows)
    half = w["q_columns"]

    def body(dn2_r, dh2_r, h1_r, attn_r, mixed_r, mid_r, n1t_r, g_r, o1_r, o2_r, lo_r, hi_r, *rest):
        turn, outs = rest[:-9], rest[-9:]
        dh1, d_mixed, d_mid, d_o1, d_o2, d_lrd, d_lru, d_gain, sum_o = outs
        at = pl.program_id(0)
        part, gain_two = norm_back(h1_r[...], g_r[2:3], dn2_r[...])
        total = part + dh2_r[...]
        dh1[...] = total
        d_attn, gain_one = norm_back(attn_r[...].astype(wide), g_r[1:2], total)
        d_attn = d_attn.astype(low)
        add_to(sum_o, product(across(d_attn, turn), mixed_r[...]), at)
        d_mixed[:, :half] = product(d_attn, o1_r[...]).astype(low)
        d_mixed[:, half:] = product(d_attn, o2_r[...]).astype(low)
        d_lr = total.astype(low)
        d_middle = product(d_lr, hi_r[:, slot : slot + LANES])[:, :rank].astype(low)
        d_mid[...] = d_middle
        add_to(d_lru, product(across(d_lr, turn), mid_r[...]), at)
        add_to(d_lrd, product(n1t_r[...], d_middle), at)
        add_to(d_gain, gain_rows([(1, gain_one), (2, gain_two)], width), at)

        @pl.when(at == count - 1)
        def _():
            d_o1[...] = sum_o[:, :half].astype(low)
            d_o2[...] = sum_o[:, half:].astype(low)

    return run(
        body,
        (count,),
        [
            (dn2, (tile, width), by_row),
            (dh2, (tile, width), by_row),
            (s["h1"], (tile, width), by_row),
            (s["attn"], (tile, width), by_row),
            (s["mixed"], (tile, 2 * half), by_row),
            (s["mid"], (tile, rank), by_row),
            (s["n1t"], (width, tile), by_column),
            (g, g.shape, None),
            (w["qo"][0], (width, half), lambda i: (0, w["q_at"] + 1)),
            (w["qo"][1], (width, half), lambda i: (0, w["q_at"] + 1)),
            (w["lo"], w["lo"].shape, None),
            (w["hi"], w["hi"].shape, None),
            *turn_spec(w),
        ],
        [
            ((rows, width), wide, (tile, width), by_row),
            ((rows, 2 * half), low, (tile, 2 * half), by_row),
            ((rows, rank), low, (tile, rank), by_row),
            ((width, half), low, (width, half), None),
            ((width, half), low, (width, half), None),
            ((width, rank), wide, (width, rank), None),
            ((width, rank), wide, (width, rank), None),
            ((GAIN_ROWS, width), wide, (GAIN_ROWS, width), None),
        ],
        scratch=[pltpu.VMEM((width, 2 * half), wide)],
        flops=4 * rows * width * (2 * half + 2 * rank),
    )


def attend_back(d_mixed, s, pieces, w, shared):
    lowest, head_width, steps = (shared[k] for k in ("lowest", "hd", "steps"))
    rows, every = d_mixed.shape
    here = rows // steps
    hops = len(pieces) - 1
    heads = every // head_width

    def body(q_r, low_r, dm_r, qpre_r, cos_r, sin_r, qk_r, *rest):
        piece_refs, rest = rest[: hops + 1], rest[hops + 1 :]
        d_qpre, d_own, d_gain = rest[:3]
        edges, (sum_k, sum_v) = rest[3 : 3 + hops], rest[3 + hops :]
        step, head = pl.program_id(0), pl.program_id(1)
        keys = jnp.concatenate([p[:, :head_width] for p in piece_refs], axis=0)
        values = jnp.concatenate([p[:, head_width:] for p in piece_refs], axis=0)
        query, d_m = q_r[...], dm_r[...]
        probs = window_probs(query, keys, low_r[...], hops * here)
        add_to(sum_v, product(probs.astype(low).T, d_m), head)
        d_probs = product_nt(d_m, values)
        d_scores = probs * (d_probs - jnp.sum(probs * d_probs, axis=-1, keepdims=True))
        d_scores = d_scores.astype(low)
        add_to(sum_k, product(d_scores.T, query), head)
        d_query = product(d_scores, keys) * head_width ** (-0.5)
        d_pre, gain = norm_back(
            qpre_r[...].astype(wide), qk_r[0:1], rotate_back(d_query, cos_r[...], sin_r[...])
        )
        d_qpre[...] = d_pre.astype(low)
        add_to(d_gain, gain_rows([(0, gain)], head_width), step * heads + head)

        @pl.when(head == heads - 1)
        def _():
            for at in range(hops):
                part = slice(at * here, (at + 1) * here)
                edges[at][:, :head_width] = sum_k[part].astype(low)
                edges[at][:, head_width:] = sum_v[part].astype(low)
            d_own[:, :head_width] = sum_k[hops * here :]
            d_own[:, head_width:] = sum_v[hops * here :]

    both = 2 * head_width
    outs = run(
        body,
        (steps, heads),
        [
            (s["queries"], (here, head_width), lambda i, h: (i, h)),
            (lowest, (here, 1), lambda i, h: (i, 0)),
            (d_mixed, (here, head_width), lambda i, h: (i, h)),
            (s["qpre"], (here, head_width), lambda i, h: (i, h)),
            (shared["cos"], (here, head_width // 2), lambda i, h: (i, 0)),
            (shared["sin"], (here, head_width // 2), lambda i, h: (i, 0)),
            (w["qk"], w["qk"].shape, None),
        ]
        + [(p, (here, both), lambda i, h: (i, 0)) for p in pieces],
        [
            ((rows, every), low, (here, head_width), lambda i, h: (i, h)),
            ((rows, both), wide, (here, both), lambda i, h: (i, 0)),
            ((GAIN_ROWS, head_width), wide, (GAIN_ROWS, head_width), None),
        ]
        + [((rows, both), low, (here, both), lambda i, h: (i, 0)) for _ in range(hops)],
        scratch=[pltpu.VMEM(((hops + 1) * here, head_width), wide)] * 2,
        flops=10 * rows * every * (hops + 1) * here,
    )
    return outs[0], outs[1], outs[2], outs[3:]


def query_back(d_qpre, d_mid, s, w, shared):
    rank, slot = shared["rank"], w["slot"]
    rows, every = d_qpre.shape
    width = s["n1t"].shape[0]
    tile, count = row_tiles(rows)
    half = every // 2

    def body(dq_r, dmid_r, n1t_r, q1_r, q2_r, lo_r, dn1, d_q1, d_q2, sum_q):
        at = pl.program_id(0)
        value = dq_r[...]
        dn1[...] = (
            product_nt(value[:, :half], q1_r[...])
            + product_nt(value[:, half:], q2_r[...])
            + product_nt(dmid_r[...], lo_r[:, slot : slot + LANES][:, :rank])
        )
        add_to(sum_q, product(n1t_r[...], value), at)

        @pl.when(at == count - 1)
        def _():
            d_q1[...] = sum_q[:, :half].astype(low)
            d_q2[...] = sum_q[:, half:].astype(low)

    return run(
        body,
        (count,),
        [
            (d_qpre, (tile, every), by_row),
            (d_mid, (tile, rank), by_row),
            (s["n1t"], (width, tile), by_column),
            (w["qo"][0], (width, half), lambda i: (0, w["q_at"])),
            (w["qo"][1], (width, half), lambda i: (0, w["q_at"])),
            (w["lo"], w["lo"].shape, None),
        ],
        [
            ((rows, width), wide, (tile, width), by_row),
            ((width, half), low, (width, half), None),
            ((width, half), low, (width, half), None),
        ],
        scratch=[pltpu.VMEM((width, every), wide)],
        flops=4 * rows * width * every,
    )


def key_back(d_own, received, dn1, dh1, x, s, g, w, shared):
    head_width = shared["hd"]
    rows, width = x.shape
    tile, count = row_tiles(rows)
    both = 2 * head_width
    kv_at = w["slot"] - head_width
    hops = len(received)

    def body(own_r, dn1_r, dh1_r, x_r, kpre_r, n1t_r, cos_r, sin_r, qk_r, g_r, lo_r, hi_r, *rest):
        edges, (dx, d_kv, d_gain, d_key_gain) = rest[:hops], rest[hops:]
        at = pl.program_id(0)
        total = own_r[...]
        for edge in edges:
            total = total + edge[...].astype(wide)
        d_pre, key_gain = norm_back(
            kpre_r[...].astype(wide),
            qk_r[1:2],
            rotate_back(total[:, :head_width], cos_r[...], sin_r[...]),
        )
        d_k, d_v = d_pre.astype(low), total[:, head_width:].astype(low)
        add_to(d_kv, product(n1t_r[...], jnp.concatenate([d_k, d_v], axis=1)), at)
        d_normed = (
            dn1_r[...]
            + product_nt(d_k, lo_r[:, kv_at : kv_at + head_width])
            + product_nt(d_v, hi_r[:, kv_at : kv_at + head_width])
        )
        part, gain_zero = norm_back(x_r[...].astype(wide), g_r[0:1], d_normed)
        dx[...] = (part + dh1_r[...]).astype(low)
        add_to(d_gain, gain_rows([(0, gain_zero)], width), at)
        add_to(d_key_gain, gain_rows([(1, key_gain)], head_width), at)

    return run(
        body,
        (count,),
        [
            (d_own, (tile, both), by_row),
            (dn1, (tile, width), by_row),
            (dh1, (tile, width), by_row),
            (x, (tile, width), by_row),
            (s["kpre"], (tile, head_width), by_row),
            (s["n1t"], (width, tile), by_column),
            (shared["cos"], (tile, head_width // 2), by_row),
            (shared["sin"], (tile, head_width // 2), by_row),
            (w["qk"], w["qk"].shape, None),
            (g, g.shape, None),
            (w["lo"], w["lo"].shape, None),
            (w["hi"], w["hi"].shape, None),
        ]
        + [(edge, (tile, both), by_row) for edge in received],
        [
            ((rows, width), low, (tile, width), by_row),
            ((width, both), wide, (width, both), None),
            ((GAIN_ROWS, width), wide, (GAIN_ROWS, width), None),
            ((GAIN_ROWS, head_width), wide, (GAIN_ROWS, head_width), None),
        ],
        flops=4 * rows * width * both,
    )


MESSAGE_PARTS = ("gate", "up", "down", "q", "o", "ig", "ip", "kv", "slot")


def whole_run(body, section, ins, outs):
    def spec(shape):
        return pl.BlockSpec(shape, lambda i: (0,) * len(shape))

    return pl.pallas_call(
        body,
        grid=(1,),
        in_specs=[pl.BlockSpec(memory_space=pltpu.SMEM)] + [spec(value.shape) for value in ins],
        out_specs=[spec(shape) for shape, _ in outs],
        out_shape=[jax.ShapeDtypeStruct(shape, dtype) for shape, dtype in outs],
        compiler_params=pltpu.CompilerParams(vmem_limit_bytes=VMEM_BYTES),
    )(section, *ins)


def by_section(section_ref, function):
    @pl.when(section_ref[0] == 0)
    def _():
        function(0)

    @pl.when(section_ref[0] != 0)
    def _():
        function(1)


def message_columns(sizes):
    places, start = {name: [] for name in MESSAGE_PARTS}, 0
    tile = min(TILE, sizes["gate"])
    for at in range(0, sizes["gate"], tile):
        for name in MESSAGE_PARTS[:3]:
            places[name].append((start, at, tile))
            start += tile
    for name in MESSAGE_PARTS[3:]:
        places[name].append((start, 0, sizes[name]))
        start += sizes[name]
    return places, start


def pack_shards(section, wholes, pairs, sizes):
    places, total = message_columns(sizes)
    names = list(wholes)
    rows = wholes[names[0]].shape[0]
    ins = [wholes[n] for n in names] + [p for n in pairs for p in pairs[n]]

    def body(section_r, *refs):
        whole_refs = dict(zip(names, refs))
        pair_refs, start = {}, len(names)
        for name in pairs:
            pair_refs[name] = refs[start : start + 2]
            start += 2
        outs = refs[start:]

        def write(section):
            for out, half in ((outs[0], section), (outs[1], 1 - section)):
                for name, spots in places.items():
                    for to, at, size in spots:
                        if name in pair_refs:
                            value = pair_refs[name][half][:, at : at + size]
                        else:
                            begin = half * sizes[name] + at
                            value = whole_refs[name][:, begin : begin + size]
                        out[:, to : to + size] = value

        by_section(section_r, write)

    return whole_run(body, section, ins, [((rows, total), low)] * 2)


def split_layers(section, kept, received, cuts):
    rows, total = kept.shape

    def body(section_r, kept_r, received_r, *outs):
        def write(section):
            zero, one = ((kept_r, received_r), (received_r, kept_r))[section]
            for out, (start, stop) in zip(outs, cuts):
                out[...] = zero[:, start:stop]
            outs[-1][...] = one[...]

        by_section(section_r, write)

    outs = [((rows, stop - start), low) for start, stop in cuts] + [((rows, total), low)]
    return whole_run(body, section, [kept, received], outs)


def join_layers(section, pieces, cuts, one):
    def body(section_r, *refs):
        piece_refs, one_r, kept, sent = refs[: len(cuts)], refs[-3], refs[-2], refs[-1]

        def write(section):
            zero_out, one_out = ((kept, sent), (sent, kept))[section]
            for ref, (start, stop) in zip(piece_refs, cuts):
                zero_out[:, start:stop] = ref[...].astype(wide)
            one_out[...] = one_r[...].astype(wide)

        by_section(section_r, write)

    return whole_run(body, section, [*pieces, one], [(one.shape, wide)] * 2)


def unpack_shards(section, kept, received, sizes):
    places, _ = message_columns(sizes)
    rows = kept.shape[0]

    def body(section_r, kept_r, received_r, *outs):
        def write(section):
            halves = ((kept_r, received_r), (received_r, kept_r))[section]
            for out, (name, spots) in zip(outs, places.items()):
                for half, ref in enumerate(halves):
                    for start, at, size in spots:
                        begin = half * sizes[name] + at
                        out[:, begin : begin + size] = ref[:, start : start + size]

        by_section(section_r, write)

    outs = [((rows, 2 * sizes[name]), wide) for name in places]
    return dict(zip(places, whole_run(body, section, [kept, received], outs)))


def local(
    tokens,
    layer_inputs,
    doc_lengths,
    order,
    out_grad,
    query_weight,
    key_weight,
    value_weight,
    output_weight,
    gate_weight,
    up_weight,
    down_weight,
    lowrank_down,
    lowrank_up,
    input_gate,
    input_proj,
    norm_gains,
    qk_gains,
):
    section = lax.axis_index("section")
    block_index = lax.axis_index("seq")
    first = section == 0
    micro_count = order.shape[1]
    steps = micro_count // 2
    rows_here = tokens.shape[1]
    width = tokens.shape[2]
    rows = steps * rows_here
    hops = (WINDOW - 2) // rows_here + 1
    shard_rows = query_weight.shape[1]
    head_width = key_weight.shape[2]
    head_shard = qk_gains.shape[2]
    gain_count = norm_gains.shape[1]
    shard_count = lax.axis_size("seq") * lax.axis_size("fsdp")
    shard_index = block_index * lax.axis_size("fsdp") + lax.axis_index("fsdp")
    rank = lowrank_down.shape[2]
    extra_half = input_gate.shape[2] // 2
    q_columns = query_weight.shape[2] // 2
    ff_half = gate_weight.shape[2] // 2
    slot = head_width + 2 * extra_half
    misc_columns = slot + LANES
    links = Links()
    assert 2 * head_shard <= shard_rows and gain_count < GAIN_ROWS
    assert rank + GAIN_ROWS <= LANES
    sizes = {
        "gate": ff_half,
        "up": ff_half,
        "down": ff_half,
        "q": q_columns,
        "o": q_columns,
        "ig": extra_half,
        "ip": extra_half,
        "kv": head_width,
        "slot": LANES,
    }
    q_at = 3 * ff_half // q_columns
    assert 3 * ff_half % q_columns == 0
    misc_at = 3 * ff_half + 2 * q_columns

    def choose(one, two):
        return jnp.where(first, one, two)

    section_number = section.reshape(1).astype(jnp.int32)
    qk_column = jnp.pad(qk_gains[0].reshape(1, -1), ((0, 0), (0, shard_rows - 2 * head_shard)))
    gain_block = jnp.concatenate([norm_gains[0], qk_column], axis=0).T

    def slot_of(part):
        return jnp.pad(
            jnp.concatenate([part, gain_block], axis=1),
            ((0, 0), (0, LANES - rank - gain_count - 1)),
        )

    wholes = {
        "gate": gate_weight[0],
        "up": up_weight[0],
        "down": down_weight[0].T,
        "q": query_weight[0],
        "o": output_weight[0].T,
        "ig": input_gate[0],
        "ip": input_proj[0].T,
    }
    pairs = {
        "kv": (key_weight[0], value_weight[0]),
        "slot": (slot_of(lowrank_down[0]), slot_of(lowrank_up[0].T)),
    }
    kept, sent = pack_shards(section_number, wholes, pairs, sizes)
    middle_column = 3 * (ff_half // 2)
    cuts = (
        (3 * ff_half, misc_at),
        (misc_at, misc_at + misc_columns),
        (0, middle_column),
        (middle_column, 3 * ff_half),
    )
    shard_rest, shard_yz, shard_next = split_layers(
        section_number, kept, swap_cores(sent), ((3 * ff_half, kept.shape[1]), (0, 3 * ff_half))
    )
    line = Line()

    turned = shard_index % (lax.axis_size("fsdp") * min(2, lax.axis_size("seq")))
    place = jnp.arange(2 * shard_count * head_shard)
    half_at, head_at = place // (shard_count * head_shard), place % (shard_count * head_shard)


    def qk_ordering_of(me):
        source = (
            ((head_at // head_shard) ^ me) * shard_rows + half_at * head_shard + head_at % head_shard
        )
        return (jnp.arange(width)[:, None] == source[None, :]).astype(low)

    qk_orderings = (qk_ordering_of(turned), qk_ordering_of(0))
    column = jnp.arange(width)
    source = (turned ^ (column // shard_rows)) * shard_rows + column % shard_rows
    ordering = (jnp.arange(width)[:, None] == source[None, :]).astype(low)

    def to_blocks(value):
        return product(value, ordering).astype(low)

    def from_blocks(value):
        return product_nt(value, ordering).astype(low)

    def misc_weights(layer, mine, other):
        result = {"slot": slot, "q_columns": q_columns, "turn": (None, ordering.T)[layer]}
        result["lo"], result["hi"] = choose(mine, other), choose(other, mine)
        gains = mine[:, slot + rank : slot + rank + GAIN_ROWS].T
        result["gains"] = gains.astype(wide)
        qk = product(gains, qk_orderings[layer])[gain_count]
        result["qk"] = qk.reshape(2, -1)
        return result

    def fetch(kv):
        return [from_behind(kv, distance) for distance in range(hops, 0, -1)] + [kv]

    def send_back(edges):
        return [from_behind(edge, at - hops) for at, edge in enumerate(edges)]

    def local_step(function, value, *rest):
        result = function(line.wait(value), *rest)
        line.done(result[0] if isinstance(result, (tuple, list)) else result)
        return result

    def step_all(*chains):
        for chain in chains:
            chain.step()

    weights = [None, None]
    saved = [{}, {}]

    def forward_a(layer, x):
        w, s = weights[layer], saved[layer]
        s["x"] = x
        s["n1t"], s["queries"], kv, s["qpre"], s["kpre"], s["mid"] = local_step(
            project, x, w["gains"], w, shared
        )
        s["pieces"] = fetch(kv)

    def forward_b(layer):
        w, s = weights[layer], saved[layer]
        s["mixed"] = local_step(attend, s["queries"], s["pieces"], shared)

    def forward_c(layer):
        w, s = weights[layer], saved[layer]
        s["attn"], s["h1"], s["n2"], s["n2t"] = local_step(
            attention_out, s["x"], s["mixed"], s["mid"], w["gains"], w, shared
        )

    def forward_d(layer, at, before):
        w, s = weights[layer], saved[layer]
        s["gu", at], total = local_step(ffn, s["n2"], w["yz"][at], ff_half, before)
        return total

    def forward_e(layer, total):
        w, s = weights[layer], saved[layer]
        s["ff"], s["h2t"], s["pgate"], s["mix"], s["pout"], y = local_step(
            pli, s["h1"], total, extras[layer], w["gains"], w, shared
        )
        return y

    def both_cores(value):
        return value, swap_cores(value)

    def set_misc(layer, mine, other):
        weights[layer] = misc_weights(layer, mine, other)
        line.done(weights[layer]["lo"])

    def gather(piece, order=None):
        return Gather(line, links, piece, order)

    def pieces_of(chain, spots, at=0):
        value = finish(chain)
        return [value[:, a - at : b - at] for a, b in spots]

    whole_next = lax.all_gather(shard_next, ("seq", "fsdp"), axis=0, tiled=True)
    first_far = gather(shard_rest)
    second_far = gather(shard_yz)

    own_order = line.wait(order[0])
    sequence_of = [own_order[section * steps + i] for i in range(steps)]
    other_sequence = [own_order[(1 - section) * steps + i] for i in range(steps)]
    lengths = jnp.stack([doc_lengths[seq] for seq in sequence_of])
    ends = jnp.cumsum(lengths, axis=1)
    positions = block_index * rows_here + jnp.arange(rows_here, dtype=jnp.int32)
    passed = positions[None, :, None] >= ends[:, None, :]
    doc_start = jnp.sum(jnp.where(passed, lengths[:, None, :], 0), axis=2)
    offsets = positions[None] - doc_start
    inverse = rope_base ** (-(jnp.arange(head_width // 2, dtype=wide) * 2.0 / head_width))
    angles = offsets.astype(wide).reshape(-1)[:, None] * inverse[None, :]
    lowest = jnp.maximum(doc_start, positions[None] - (WINDOW - 1))
    lowest = lowest - (block_index - hops) * rows_here
    shared = {
        "cos": jnp.cos(angles),
        "sin": jnp.sin(angles),
        "lowest": lowest.reshape(-1, 1),
        "hd": head_width,
        "rank": rank,
        "steps": steps,
    }

    own_extra = line.wait(layer_inputs[0])
    extra_kept = jnp.stack([own_extra[seq] for seq in sequence_of]).reshape(rows, -1)
    extra_received = swap_cores(jnp.stack([own_extra[seq] for seq in other_sequence])).reshape(
        rows, -1
    )
    extras = [choose(extra_kept, extra_received), choose(extra_received, extra_kept)]
    inputs = to_blocks(jnp.stack([tokens[seq] for seq in sequence_of]).reshape(rows, width))

    line.done(inputs)
    step_all(first_far, second_far)
    qo, m = (
        gather(v, o) for v, o in zip(pieces_of(first_far, cuts[:2], 3 * ff_half), ("one", "two"))
    )
    yz = [gather(v, o) for v, o in zip(pieces_of(second_far, cuts[2:]), ("one", "two"))]
    step_all(m, qo)
    step_all(*yz)
    m = both_cores(finish(m))
    qo = both_cores(finish(qo))
    set_misc(0, *m)
    weights[0].update(qo=qo, q_at=0)
    forward_a(0, inputs)
    weights[0]["yz"] = both_cores(finish(*yz))
    forward_b(0)
    forward_c(0)
    total = forward_d(0, 0, None)
    whole_next = both_cores(line.wait(whole_next))
    total = forward_d(0, 1, total)
    middle = forward_e(0, total)
    middle_own = line.done(from_blocks(line.wait(middle)))
    set_misc(1, *(value[:, misc_at:] for value in whole_next))
    weights[1].update(qo=whole_next, q_at=q_at, yz=whole_next)
    forward_a(1, middle_own)
    forward_b(1)
    forward_c(1)
    total = forward_d(1, 0, None)
    total = forward_d(1, 1, total)
    last = forward_e(1, total)
    grad_last = lax.dynamic_slice_in_dim(
        line.wait(out_grad), section * steps, steps, 0
    ).reshape(rows, width)

    def by_step(layer_one, layer_two):
        mine = choose(layer_one, layer_two).reshape(steps, rows_here, width)
        other = swap_cores(choose(layer_two, layer_one)).reshape(steps, rows_here, width)
        return jnp.concatenate([choose(mine, other), choose(other, mine)], axis=0)

    grads = [{}, {}]

    def back_a(layer, grad):
        w, s, d = weights[layer], saved[layer], grads[layer]
        d["dh2"], d["dff"], d["dfft"], d["ig"], d["ip"], d["ga"] = local_step(
            pli_back, grad, s, extras[layer], w["gains"], w, shared
        )

    def back_b(layer, at, before):
        w, s, d = weights[layer], saved[layer], grads[layer]
        d["yz", at], total = local_step(
            ffn_back, d["dff"], d["dfft"], s["n2t"], s["gu", at], w["yz"][at], before
        )
        return total

    def back_c(layer, dn2):
        w, s, d = weights[layer], saved[layer], grads[layer]
        d["dh1"], d["dm"], d["dmid"], d["o", 0], d["o", 1], d["lrd"], d["lru"], d["gb"] = (
            local_step(attention_out_back, dn2, d["dh2"], s, w["gains"], w, shared)
        )

    def back_d(layer):
        w, s, d = weights[layer], saved[layer], grads[layer]
        d["dq"], d["own"], d["gq"], edges = local_step(
            attend_back, d["dm"], s, s["pieces"], w, shared
        )
        d["edges"] = send_back(edges)

    def back_e(layer):
        w, s, d = weights[layer], saved[layer], grads[layer]
        d["dn1"], d["q", 0], d["q", 1] = local_step(query_back, d["dq"], d["dmid"], s, w, shared)

    def back_f(layer):
        w, s, d = weights[layer], saved[layer], grads[layer]
        dx, d["kv"], d["gc"], d["gk"] = local_step(
            key_back, d["own"], d["edges"], d["dn1"], d["dh1"], s["x"], s, w["gains"], w, shared
        )
        return dx

    def misc_grads(layer):
        d = grads[layer]
        qk = (d["gq"] + d["gk"])[:2].reshape(1, -1).astype(low)
        row = jnp.arange(GAIN_ROWS)[:, None]
        gains = jnp.where(
            row == gain_count, product_nt(qk, qk_orderings[layer]), d["ga"] + d["gb"] + d["gc"]
        ).astype(low)
        gains = gains.T if layer == 0 else product_nt(ordering.T, gains).astype(low)

        def misc(at):
            last = jnp.concatenate([d[("lrd", "lru")[at]].astype(low), gains], axis=1)
            return jnp.concatenate(
                [
                    halves(d["kv"])[at].astype(low),
                    jnp.pad(last, ((0, 0), (0, LANES - last.shape[1]))),
                ],
                axis=1,
            )

        lo, hi = misc(0), misc(1)
        return choose(lo, hi), choose(hi, lo)

    def extra_grads(layer):
        d = grads[layer]
        lo, hi = (
            jnp.concatenate([halves(d["ig"])[at], halves(d["ip"])[at]], axis=1).astype(low)
            for at in range(2)
        )
        return choose(lo, hi), choose(hi, lo)

    def halves(value):
        middle = value.shape[1] // 2
        return value[:, :middle], value[:, middle:]

    def sum_of(mine, received, order, with_far=False):
        return Sum(line, links, mine, received, order, with_far)

    def yz_sums(layer, received):
        mine = grads[layer]["yz", 0]
        return [
            sum_of([mine[:, a:b]], [received[:, a:b]], o) for (a, b), o in zip(cuts[2:], ("one", "two"))
        ]

    def far_sum(*chains):
        value = jnp.concatenate([chain.result().astype(low) for chain in chains], axis=1)
        return lax.psum_scatter(
            line.done(value), "seq", axis_index_groups=links.groups, scatter_dimension=0, tiled=True
        )

    back_a(1, grad_last)
    dn2 = back_b(1, 1, None)
    yz_received = swap_cores(grads[1]["yz", 1])
    extra_mine, extra_other = extra_grads(1)
    extra_got = swap_cores(extra_other)
    dn2 = back_b(1, 0, dn2)
    yz = yz_sums(1, yz_received)
    back_c(1, dn2)
    o_received = swap_cores(grads[1]["o", 1])
    back_d(1)
    step_all(*yz)
    back_e(1)
    q_received = swap_cores(grads[1]["q", 1])
    grad_middle = back_f(1)
    qo = sum_of(
        [grads[1]["q", 0], grads[1]["o", 0], extra_mine], [q_received, o_received, extra_got], "one"
    )
    back_a(0, line.done(to_blocks(line.wait(grad_middle))))
    m_mine, m_other = misc_grads(1)
    m = sum_of([m_mine], [swap_cores(m_other)], "two")
    dn2 = back_b(0, 1, None)
    yz_received = swap_cores(grads[0]["yz", 1])
    extra_mine, extra_other = extra_grads(0)
    extra_got = swap_cores(extra_other)
    step_all(qo, m)
    dn2 = back_b(0, 0, dn2)
    sum_next = far_sum(*yz, qo, m)
    yz = yz_sums(0, yz_received)
    back_c(0, dn2)
    o_received = swap_cores(grads[0]["o", 1])
    back_d(0)
    step_all(*yz)
    back_e(0)
    q_received = swap_cores(grads[0]["q", 1])
    sum_yz = far_sum(*yz)
    qo = sum_of(
        [grads[0]["q", 0], grads[0]["o", 0], extra_mine],
        [q_received, o_received, extra_got],
        "one",
        True,
    )
    grad_tokens = back_f(0)
    m_mine, m_other = misc_grads(0)
    m = sum_of([m_mine], [swap_cores(m_other)], "two", True)
    activations = by_step(middle_own, last)
    input_grads = by_step(from_blocks(grad_tokens), grad_middle)
    step_all(qo, m, qo, m, qo, m)
    pieces = [sum_yz, qo.result(), m.result()]

    ends = [sum(v.shape[1] for v in pieces[: at + 1]) for at in range(len(pieces))]
    spots = list(zip([0] + ends, ends))
    kept, sent = join_layers(section_number, pieces, spots, sum_next)
    parts = unpack_shards(section_number, kept, swap_cores(sent), sizes)
    last_slot = parts["slot"]
    gains = last_slot[:, rank : rank + GAIN_ROWS].T
    return tuple(
        value[None]
        for value in (
            activations,
            input_grads,
            parts["q"],
            parts["kv"][:, :head_width],
            parts["kv"][:, head_width:],
            parts["o"].T,
            parts["gate"],
            parts["up"],
            parts["down"].T,
            last_slot[:, :rank],
            last_slot[:, LANES : LANES + rank].T,
            parts["ig"],
            parts["ip"].T,
            gains[:gain_count],
            gains[gain_count, : 2 * head_shard].reshape(2, head_shard),
        )
    )


def solution(mesh):
    shards = ("seq", "fsdp")
    rows_cut = P("section", shards, None)
    columns_cut = P("section", None, shards)
    steps_cut = P("section", "fsdp", "seq", None)
    in_specs = (
        P("fsdp", "seq", None),
        steps_cut,
        P("fsdp", None),
        P("fsdp", None),
        P("fsdp", "seq", None),
        rows_cut,
        rows_cut,
        rows_cut,
        columns_cut,
        rows_cut,
        rows_cut,
        columns_cut,
        rows_cut,
        columns_cut,
        rows_cut,
        columns_cut,
        columns_cut,
        columns_cut,
    )
    out_specs = (
        steps_cut,
        steps_cut,
        rows_cut,
        rows_cut,
        rows_cut,
        columns_cut,
        rows_cut,
        rows_cut,
        columns_cut,
        rows_cut,
        columns_cut,
        rows_cut,
        columns_cut,
        columns_cut,
        columns_cut,
    )
    return jax.shard_map(local, mesh=mesh, in_specs=in_specs, out_specs=out_specs, check_vma=False)
```
